256 devices in a mesh: dp: 64 (over x, z_lo, y, core), feat: 4 (over z_hi).
Axes of the slice: x: 4, y: 4, z: 8 (z_hi: 4, z_lo: 2; z = z_hi * 2 + z_lo), core: 2. Of those that a mesh axis runs over, the one named last changes fastest.
Arguments:
- view_one: bfloat16 [8192, 8192], P('dp', 'feat'), may hold values from -1000 to 1000
- view_two: bfloat16 [8192, 8192], P('dp', 'feat'), may hold values from -1000 to 1000
Outputs:
- grad_one: bfloat16 [8192, 8192], P('dp', 'feat')
- grad_two: bfloat16 [8192, 8192], P('dp', 'feat')
The draws below stay inside these ranges and needn't reach their ends.
All inputs are finite; a program needn't handle non-finite values.
Results may differ from the reference program's by a relative error of at most 0.0065.
Values may be sent and summed in bfloat16 or wider, within the bound.
No kernel may reach another device: no remote copies, remote signals or barrier semaphores. Data moves between devices by JAX's collectives and lax.ppermute only.
A program may use at most 64 MiB of HBM per device.

```python
import math
import jax
import jax.numpy as jnp
from jax import lax

FEAT = 8192
BATCH = 8192
GRID_I = 8
GRID_J = 8
TILE_I = 1024
TILE_J = 1024


def common_part(key):
    keys = jax.random.split(key, 4)
    latent = jnp.clip(jax.random.normal(keys[0], (BATCH, FEAT), jnp.float32), -6.0, 6.0)
    factors = jnp.clip(jax.random.normal(keys[1], (BATCH, 4), jnp.float32), -6.0, 6.0)
    loadings = jnp.clip(0.15 * jax.random.normal(keys[2], (4, FEAT), jnp.float32), -0.6, 0.6)
    for factor_index in range(4):
        latent = latent + factors[:, factor_index:factor_index + 1] * loadings[factor_index][None, :]
    kinship = jax.random.uniform(keys[3], (FEAT,), jnp.float32, 0.75, 0.97)
    position = jnp.arange(BATCH, dtype=jnp.float32)[:, None] / (BATCH - 1.0)
    rising = math.log(3.0) * position
    row_scale = jnp.exp(rising)
    return (latent, kinship, row_scale)


def view_part(key, shared):
    latent, kinship, row_scale = shared
    keys = jax.random.split(key, 3)
    noise = jnp.clip(jax.random.normal(keys[0], (BATCH, FEAT), jnp.float32), -6.0, 6.0)
    scale = jnp.exp(jax.random.uniform(keys[1], (FEAT,), jnp.float32, math.log(0.3), math.log(3.0)))
    offset = scale * jax.random.uniform(keys[2], (FEAT,), jnp.float32, -1.0, 1.0)
    mixed = kinship * latent + jnp.sqrt(1.0 - kinship * kinship) * noise
    return (offset + scale * row_scale * mixed).astype(jnp.bfloat16)


def draw_view_one(key, part):
    shared = common_part(key)
    key = jax.random.fold_in(key, 11)
    return view_part(key, shared)


def draw_view_two(key, part):
    shared = common_part(key)
    key = jax.random.fold_in(key, 23)
    return view_part(key, shared)


def setup_inputs(seed: int = 0) -> dict:
    splits = jax.random.split(jax.random.key(seed), 3)
    return {
        "view_one": draw_view_one(jax.random.fold_in(splits[2], 71), 0),
        "view_two": draw_view_two(jax.random.fold_in(splits[2], 71), 0),
    }


EPSILON = 1e-05
OFF_WEIGHT = 0.0051

def moments(values):
    count = values.shape[0]
    mean_value = lax.optimization_barrier(jnp.sum(values, 0)) / count
    variance = lax.optimization_barrier(jnp.sum(values * values, 0)) / count - mean_value * mean_value
    return (mean_value, lax.rsqrt(variance + EPSILON))

def slope_tile(correlation, row_index, col_index):
    same = row_index[:, None] == col_index[None, :]
    return jnp.where(same, -2.0 * (1.0 - correlation), 2.0 * OFF_WEIGHT * correlation)

def reference(view_one, view_two):
    count = view_one.shape[0]
    width = view_one.shape[1]
    first = view_one.astype(jnp.float32)
    second = view_two.astype(jnp.float32)
    mean_one, inverse_one = moments(first)
    mean_two, inverse_two = moments(second)
    norm_one = (first - mean_one) * inverse_one
    norm_two = (second - mean_two) * inverse_two
    round_one = norm_one.astype(jnp.bfloat16)
    round_two = norm_two.astype(jnp.bfloat16)
    correlation = lax.dot_general(round_one, round_two, (((0,), (0,)), ((), ())), preferred_element_type=jnp.float32) / count
    index = jnp.arange(width, dtype=jnp.int32)
    grad_full = slope_tile(correlation, index, index).astype(jnp.bfloat16)
    pieces_two = round_two.reshape(count, GRID_J, TILE_J).transpose(1, 0, 2)
    grad_cols = grad_full.reshape(width, GRID_J, TILE_J).transpose(1, 0, 2)

    def step_one(carry, pair):
        block_two, block_grad = pair
        term = lax.dot_general(block_two, block_grad, (((1,), (1,)), ((), ())), preferred_element_type=jnp.float32)
        term = lax.optimization_barrier(term.astype(jnp.bfloat16)).astype(jnp.float32)
        return (carry + term, None)
    back_one, _ = lax.scan(step_one, jnp.zeros((count, width), jnp.float32), (pieces_two, grad_cols))
    pieces_one = round_one.reshape(count, GRID_I, TILE_I).transpose(1, 0, 2)
    grad_rows = grad_full.reshape(GRID_I, TILE_I, width)

    def step_two(carry, pair):
        block_one, block_grad = pair
        term = jnp.dot(block_one, block_grad, preferred_element_type=jnp.float32)
        term = lax.optimization_barrier(term.astype(jnp.bfloat16)).astype(jnp.float32)
        return (carry + term, None)
    back_two, _ = lax.scan(step_two, jnp.zeros((count, width), jnp.float32), (pieces_one, grad_rows))
    proj_one = lax.optimization_barrier(jnp.sum(back_one * norm_one, 0)) / count
    proj_two = lax.optimization_barrier(jnp.sum(back_two * norm_two, 0)) / count
    grad_one = (inverse_one * (back_one - norm_one * proj_one)).astype(jnp.bfloat16)
    grad_two = (inverse_two * (back_two - norm_two * proj_two)).astype(jnp.bfloat16)
    return (grad_one, grad_two)
```

```python
import itertools

import jax
import jax.numpy as jnp
from jax import lax
from jax.sharding import Mesh
from jax.sharding import PartitionSpec as P

EPSILON = 1e-05
OFF_WEIGHT = 0.0051
SIZES = (4, 2, 4, 2, 4)
AXES = ("x", "zl", "y", "c", "zh")
COLS = ("zh", "zl", "c")


def device(x, zl, y, c, zh):
    return (((x * 2 + zl) * 4 + y) * 2 + c) * 4 + zh


def pairs_one(k, back=False):
    out = []
    for x, zl, y, c, zh in itertools.product(*map(range, SIZES)):
        s = (zl * 2 + c + k) % 4
        a, b = device(x, zl, y, c, zh), device(zh, y // 2, s, y % 2, x)
        out.append((b, a) if back else (a, b))
    return out


def pairs_two(k):
    out = []
    for x, zl, y, c, zh in itertools.product(*map(range, SIZES)):
        q = (zl * 2 + c) ^ k
        out.append((device(x, zl, y, c, zh), device(x, q // 2, y, q % 2, zh)))
    return out


def shift(k):
    return [(i, (i + k) % 4) for i in range(4)]


def pick(blocks, index):
    return lax.dynamic_index_in_dim(blocks, index, 0, keepdims=False)


def put(buffer, piece, index, axis=0):
    return lax.dynamic_update_index_in_dim(buffer, piece, index, axis)


def scatter_sum4(blocks, axis, me):
    total = pick(blocks, me).astype(jnp.float32)
    for k in (1, 2, 3):
        total += lax.ppermute(pick(blocks, (me + k) % 4), axis, shift(k)).astype(jnp.float32)
    return total.astype(jnp.bfloat16)


def local(view_one, view_two):
    x, y = lax.axis_index("x"), lax.axis_index("y")
    zl, c, zh = lax.axis_index("zl"), lax.axis_index("c"), lax.axis_index("zh")
    q = zl * 2 + c
    rows = view_one.shape[0]
    width = view_one.shape[1] // 4
    count = rows * 64
    sub_one = view_one.reshape(rows, 4, width).transpose(1, 0, 2)
    sub_two = view_two.reshape(rows, 4, width).transpose(1, 0, 2)
    with jax.named_scope("relayout"):
        own_two = jnp.zeros((4, rows, width), view_two.dtype)
        for k in range(4):
            piece = pick(sub_two, q ^ k)
            if k:
                piece = lax.ppermute(piece, AXES, pairs_two(k))
            own_two = put(own_two, piece, q ^ k)
        own_one = jnp.zeros((4, rows, width), view_one.dtype)
        for k in range(4):
            piece = lax.ppermute(pick(sub_one, (q + k) % 4), AXES, pairs_one(k))
            own_one = put(own_one, piece, (y - k) % 4)
    with jax.named_scope("gather_one"):
        first = lax.all_gather(own_one.reshape(4 * rows, width), COLS, tiled=True)
    with jax.named_scope("gather_two"):
        full = jnp.zeros((4, 4, 2, 2 * rows, width), view_two.dtype)
        halves = own_two.reshape(2, 2 * rows, width)
        a = [halves[0]] + [lax.ppermute(halves[0], "x", shift(k)) for k in (1, 2, 3)]
        b = [halves[1]] + [lax.ppermute(halves[1], "y", shift(k)) for k in (1, 2, 3)]
        buf_a = jnp.zeros((4, 2 * rows, width), view_two.dtype)
        buf_b = jnp.zeros((4, 2 * rows, width), view_two.dtype)
        for k in range(4):
            buf_a = put(buf_a, a[k], (x - k) % 4)
            buf_b = put(buf_b, b[k], (y - k) % 4)
        for k in range(4):
            got_a = lax.ppermute(buf_a, "y", shift(k)) if k else buf_a
            got_b = lax.ppermute(buf_b, "x", shift(k)) if k else buf_b
            full = lax.dynamic_update_slice(full, got_a[:, None, None], (0, (y - k) % 4, 0, 0, 0))
            full = lax.dynamic_update_slice(full, got_b[None, :, None], ((x - k) % 4, 0, 1, 0, 0))
        second = full.reshape(count, width)
    with jax.named_scope("moments"):
        f, s = first.astype(jnp.float32), second.astype(jnp.float32)
        mean_one, mean_two = jnp.sum(f, 0) / count, jnp.sum(s, 0) / count
        inv_one = lax.rsqrt(jnp.sum(f * f, 0) / count - mean_one * mean_one + EPSILON)
        inv_two = lax.rsqrt(jnp.sum(s * s, 0) / count - mean_two * mean_two + EPSILON)
    with jax.named_scope("correlate"):
        raw = lax.dot_general(
            first, second, (((0,), (0,)), ((), ())), preferred_element_type=jnp.float32
        )
        corr = (raw / count - mean_one[:, None] * mean_two[None, :]) * (
            inv_one[:, None] * inv_two[None, :]
        )
        row_index = (x * 4 + y) * width + jnp.arange(width, dtype=jnp.int32)
        col_index = (zh * 4 + q) * width + jnp.arange(width, dtype=jnp.int32)
        same = row_index[:, None] == col_index[None, :]
        slope = jnp.where(same, -2.0 * (1.0 - corr), 2.0 * OFF_WEIGHT * corr)
        proj_one = jnp.sum(slope * corr, 1) * inv_one * inv_one
        proj_two = jnp.sum(slope * corr, 0) * inv_two * inv_two
        tile = (slope * (inv_one[:, None] * inv_two[None, :])).astype(jnp.bfloat16)
        tile32 = tile.astype(jnp.float32)
        const_one = mean_one * proj_one - jnp.sum(tile32 * mean_two[None, :], 1)
        const_two = mean_two * proj_two - jnp.sum(tile32 * mean_one[:, None], 0)
    with jax.named_scope("back_one"):
        part_one = lax.dot_general(
            second, tile, (((1,), (1,)), ((), ())), preferred_element_type=jnp.float32
        )
        part_one = (part_one - f * proj_one + const_one).astype(jnp.bfloat16)
    with jax.named_scope("back_two"):
        part_two = jnp.dot(first, tile, preferred_element_type=jnp.float32)
        part_two = (part_two - s * proj_two + const_two).astype(jnp.bfloat16)
    with jax.named_scope("scatter_one"):
        grad_one = lax.psum_scatter(part_one, COLS, tiled=True)
    with jax.named_scope("scatter_two"):
        parts = part_two.reshape(4, 4, 2, 2 * rows, width)
        half_a = scatter_sum4(parts[:, :, 0].transpose(1, 0, 2, 3), "y", y)
        half_b = scatter_sum4(parts[:, :, 1], "x", x)
        half_a = scatter_sum4(half_a, "x", x)
        half_b = scatter_sum4(half_b, "y", y)
        grad_two = jnp.concatenate([half_a, half_b], 0)
    with jax.named_scope("relayout_back"):
        blocks_two = grad_two.reshape(4, rows, width)
        blocks_one = grad_one.reshape(4, rows, width)
        out_one = jnp.zeros((4, rows, width), jnp.bfloat16)
        out_two = jnp.zeros((4, rows, width), jnp.bfloat16)
        for k in range(4):
            piece = pick(blocks_two, q ^ k)
            if k:
                piece = lax.ppermute(piece, AXES, pairs_two(k))
            out_two = put(out_two, piece, q ^ k)
            piece = lax.ppermute(pick(blocks_one, (y - k) % 4), AXES, pairs_one(k, True))
            out_one = put(out_one, piece, (q + k) % 4)
        out_one = out_one.transpose(1, 0, 2).reshape(rows, 4 * width)
        out_two = out_two.transpose(1, 0, 2).reshape(rows, 4 * width)
    return out_one, out_two


def solution(mesh):
    grid = Mesh(mesh.devices.reshape(SIZES), AXES)
    spec = P(("x", "zl", "y", "c"), "zh")
    return jax.shard_map(
        local, mesh=grid, in_specs=(spec, spec), out_specs=(spec, spec), check_vma=False
    )
```

```python
import functools
import itertools

import jax
import jax.numpy as jnp
from jax import lax
from jax.experimental import pallas as pl
from jax.experimental.pallas import tpu as pltpu
from jax.sharding import Mesh
from jax.sharding import PartitionSpec as P

EPSILON = 1e-05
OFF_WEIGHT = 0.0051
SIZES = (4, 2, 4, 2, 4)
AXES = ("x", "zl", "y", "c", "zh")
COLS = ("zh", "zl", "c")
VMEM = pltpu.VMEM
SMEM = pltpu.SMEM


def device(x, zl, y, c, zh):
    return (((x * 2 + zl) * 4 + y) * 2 + c) * 4 + zh


def near(k):
    out = []
    for x, zl, y, c, zh in itertools.product(*map(range, SIZES)):
        q = (zl * 2 + c) ^ k
        out.append((device(x, zl, y, c, zh), device(x, q // 2, y, q % 2, zh)))
    return out


def turn(back=False):
    out = []
    for x, zl, y, c, zh in itertools.product(*map(range, SIZES)):
        a, b = device(x, zl, y, c, zh), device(zh, y // 2, zl * 2 + c, y % 2, x)
        out.append((b, a) if back else (a, b))
    return out


def shift(k):
    return [(i, (i + k) % 4) for i in range(4)]


def spec(space=VMEM):
    return pl.BlockSpec(memory_space=space)


def split_kernel(q_ref, one, two, *outs):
    q = q_ref[0]
    width = one.shape[1] // 4
    for k, out in enumerate(outs):
        cols = pl.ds(pl.multiple_of((q ^ k) * width, width), width)
        out[0] = one[:, cols]
        out[1] = two[:, cols]


def split(q, one, two):
    rows, width = one.shape[0], one.shape[1] // 4
    shape = jax.ShapeDtypeStruct((2, rows, width), one.dtype)
    return pl.pallas_call(
        split_kernel,
        out_shape=[shape] * 4,
        in_specs=[spec(SMEM), spec(), spec()],
        out_specs=[spec()] * 4,
        name="split",
    )(q, one, two)


def join_kernel(q_ref, p0, p1, p2, p3, one, two):
    q = q_ref[0]
    rows = p0.shape[1]
    for k, piece in enumerate((p0, p1, p2, p3)):
        at = pl.ds(pl.multiple_of((q ^ k) * rows, rows), rows)
        one[at, :] = piece[0]
        two[at, :] = piece[1]


def join(q, pieces):
    _, rows, width = pieces[0].shape
    shape = jax.ShapeDtypeStruct((4 * rows, width), pieces[0].dtype)
    return pl.pallas_call(
        join_kernel,
        out_shape=[shape] * 2,
        in_specs=[spec(SMEM)] + [spec()] * 4,
        out_specs=[spec()] * 2,
        name="join",
    )(q, *pieces)


def unjoin_kernel(q_ref, one, two, *outs):
    q = q_ref[0]
    rows = outs[0].shape[1]
    for k, out in enumerate(outs):
        at = pl.ds(pl.multiple_of((q ^ k) * rows, rows), rows)
        out[0] = one[at, :]
        out[1] = two[at, :]


def unjoin(q, one, two):
    rows, width = one.shape[0] // 4, one.shape[1]
    shape = jax.ShapeDtypeStruct((2, rows, width), one.dtype)
    return pl.pallas_call(
        unjoin_kernel,
        out_shape=[shape] * 4,
        in_specs=[spec(SMEM), spec(), spec()],
        out_specs=[spec()] * 4,
        name="unjoin",
    )(q, one, two)


def unsplit_kernel(q_ref, p0, p1, p2, p3, one, two):
    q = q_ref[0]
    width = p0.shape[2]
    for k, piece in enumerate((p0, p1, p2, p3)):
        cols = pl.ds(pl.multiple_of((q ^ k) * width, width), width)
        one[:, cols] = piece[0]
        two[:, cols] = piece[1]


def unsplit(q, pieces):
    _, rows, width = pieces[0].shape
    shape = jax.ShapeDtypeStruct((rows, 4 * width), pieces[0].dtype)
    return pl.pallas_call(
        unsplit_kernel,
        out_shape=[shape] * 2,
        in_specs=[spec(SMEM)] + [spec()] * 4,
        out_specs=[spec()] * 2,
        name="unsplit",
    )(q, *pieces)


def column(row):
    return jnp.broadcast_to(row, (8, row.shape[1])).T[:, 0:1]


def line(col):
    return jnp.broadcast_to(col, (col.shape[0], 128)).T[0:1, :]


def correlate_kernel(steps, count, tile_ref, one, two, slope_out, turned_out, vec_out, acc, sums):
    step = pl.program_id(0)

    @pl.when(step == 0)
    def _():
        acc[...] = jnp.zeros_like(acc)
        sums[...] = jnp.zeros_like(sums)

    acc[...] += lax.dot_general(
        one[...], two[...], (((0,), (0,)), ((), ())), preferred_element_type=jnp.float32
    )
    for at, ref in ((0, one), (2, two)):
        value = ref[...].astype(jnp.float32).reshape(ref.shape[0] // 8, 8, ref.shape[1])
        sums[at] += jnp.sum(value, 0)
        sums[at + 1] += jnp.sum(value * value, 0)

    @pl.when(step == steps - 1)
    def _():
        mean_one = jnp.sum(sums[0], 0, keepdims=True) / count
        mean_two = jnp.sum(sums[2], 0, keepdims=True) / count
        square_one = jnp.sum(sums[1], 0, keepdims=True) / count
        square_two = jnp.sum(sums[3], 0, keepdims=True) / count
        inv_one = lax.rsqrt(square_one - mean_one * mean_one + EPSILON)
        inv_two = lax.rsqrt(square_two - mean_two * mean_two + EPSILON)
        corr = (acc[...] / count - column(mean_one) * mean_two) * (column(inv_one) * inv_two)
        row = lax.broadcasted_iota(jnp.int32, corr.shape, 0)
        col = lax.broadcasted_iota(jnp.int32, corr.shape, 1)
        same = jnp.logical_and(row == col, tile_ref[0] == tile_ref[1])
        slope = jnp.where(same, -2.0 * (1.0 - corr), 2.0 * OFF_WEIGHT * corr)
        weight = slope * corr
        proj_one = line(jnp.sum(weight, 1, keepdims=True))
        proj_two = jnp.sum(weight, 0, keepdims=True)
        slope_out[...] = slope.astype(jnp.bfloat16)
        turned_out[...] = slope.T.astype(jnp.bfloat16)
        vec_out[...] = jnp.concatenate(
            [mean_one, inv_one, proj_one, mean_two, inv_two, proj_two, proj_one, proj_two], 0
        )


def correlate(tile, one, two):
    count, width = one.shape
    block = 512
    steps = count // block
    square = jax.ShapeDtypeStruct((width, width), jnp.bfloat16)
    whole = pl.BlockSpec((width, width), lambda s: (0, 0))
    return pl.pallas_call(
        functools.partial(correlate_kernel, steps, count),
        grid=(steps,),
        out_shape=[square, square, jax.ShapeDtypeStruct((8, width), jnp.float32)],
        in_specs=[spec(SMEM)] + [pl.BlockSpec((block, width), lambda s: (s, 0))] * 2,
        out_specs=[whole, whole, pl.BlockSpec((8, width), lambda s: (0, 0))],
        scratch_shapes=[
            VMEM((width, width), jnp.float32),
            VMEM((4, 8, width), jnp.float32),
        ],
        cost_estimate=pl.CostEstimate(
            flops=2 * count * width * width, bytes_accessed=4 * count * width, transcendentals=0
        ),
        compiler_params=pltpu.CompilerParams(vmem_limit_bytes=40 * 2**20),
        name="correlate",
    )(tile, one, two)


def back(own, other, weight, own_at, other_at, vec):
    mean_own, inv_own, proj_own = (vec[own_at + i : own_at + i + 1, :] for i in range(3))
    mean_other, inv_other = (vec[other_at + i : other_at + i + 1, :] for i in range(2))
    rounded = ((other.astype(jnp.float32) - mean_other) * inv_other).astype(jnp.bfloat16)
    product = jnp.dot(rounded, weight, preferred_element_type=jnp.float32)
    norm = (own.astype(jnp.float32) - mean_own) * inv_own
    return (inv_own * (product - norm * proj_own)).astype(jnp.bfloat16)


def back_one_kernel(one, two, weight, vec, out):
    out[...] = back(one[...], two[...], weight[...], 0, 3, vec)


def back_one(one, two, weight, vec):
    count, width = one.shape
    block = 512
    rows = pl.BlockSpec((block, width), lambda s: (s, 0))
    return pl.pallas_call(
        back_one_kernel,
        grid=(count // block,),
        out_shape=jax.ShapeDtypeStruct((count, width), jnp.bfloat16),
        in_specs=[
            rows,
            rows,
            pl.BlockSpec((width, width), lambda s: (0, 0)),
            pl.BlockSpec((8, width), lambda s: (0, 0)),
        ],
        out_specs=rows,
        cost_estimate=pl.CostEstimate(
            flops=2 * count * width * width, bytes_accessed=6 * count * width, transcendentals=0
        ),
        compiler_params=pltpu.CompilerParams(vmem_limit_bytes=40 * 2**20),
        name="back_one",
    )(one, two, weight, vec)


def back_two_kernel(pos, one_a, two_a, one_b, two_b, weight, vec, *outs):
    step = pl.program_id(0)
    half_a = back(two_a[...], one_a[...], weight[...], 3, 0, vec)
    half_b = back(two_b[...], one_b[...], weight[...], 3, 0, vec)
    for k in range(4):

        @pl.when(step // 4 == k)
        def _():
            outs[k][0] = half_a
            outs[4 + k][0] = half_b


def back_two(pos, one, two, weight, vec):
    count, width = one.shape
    block = count // 32

    def at_a(s, pos):
        return (((s % 4) * 4 + (pos[1] + s // 4) % 4) * 2, 0)

    def at_b(s, pos):
        return ((((pos[0] + s // 4) % 4) * 4 + s % 4) * 2 + 1, 0)

    a, b = pl.BlockSpec((block, width), at_a), pl.BlockSpec((block, width), at_b)

    def out_spec(k):
        return pl.BlockSpec((1, block, width), lambda s, pos: (jnp.clip(s - 4 * k, 0, 3), 0, 0))

    return pl.pallas_call(
        back_two_kernel,
        grid_spec=pltpu.PrefetchScalarGridSpec(
            num_scalar_prefetch=1,
            grid=(16,),
            in_specs=[
                a,
                a,
                b,
                b,
                pl.BlockSpec((width, width), lambda s, pos: (0, 0)),
                pl.BlockSpec((8, width), lambda s, pos: (0, 0)),
            ],
            out_specs=[out_spec(k) for k in range(4)] * 2,
        ),
        out_shape=[jax.ShapeDtypeStruct((4, block, width), jnp.bfloat16)] * 8,
        cost_estimate=pl.CostEstimate(
            flops=2 * count * width * width, bytes_accessed=6 * count * width, transcendentals=0
        ),
        compiler_params=pltpu.CompilerParams(vmem_limit_bytes=40 * 2**20),
        name="back_two",
    )(pos, one, two, one, two, weight, vec)


def sum_pieces(pieces, axis):
    total = pieces[0].astype(jnp.float32)
    for k in (1, 2, 3):
        total += lax.ppermute(pieces[k], axis, shift(k)).astype(jnp.float32)
    return total.astype(jnp.bfloat16)


def pick(blocks, index):
    return lax.dynamic_index_in_dim(blocks, index, 0, keepdims=False)


def put(buffer, piece, index):
    return lax.dynamic_update_index_in_dim(buffer, piece, index, 0)


def local(view_one, view_two):
    x, y = lax.axis_index("x"), lax.axis_index("y")
    zl, c, zh = lax.axis_index("zl"), lax.axis_index("c"), lax.axis_index("zh")
    slot = zl * 2 + c
    q = slot.astype(jnp.int32).reshape(1)
    rows = view_one.shape[0]
    width = view_one.shape[1] // 4
    count = rows * 64
    with jax.named_scope("relayout"):
        pieces = list(split(q, view_one, view_two))
        for k in (1, 2, 3):
            pieces[k] = lax.ppermute(pieces[k], AXES, near(k))
        own_one, own_two = join(q, pieces)
        own_one = lax.ppermute(own_one, AXES, turn())
    with jax.named_scope("gather_one"):
        first = lax.all_gather(own_one, COLS, tiled=True)
    with jax.named_scope("gather_two"):
        halves = own_two.reshape(2, 2 * rows, width)
        a = [halves[0]] + [lax.ppermute(halves[0], "x", shift(k)) for k in (1, 2, 3)]
        b = [halves[1]] + [lax.ppermute(halves[1], "y", shift(k)) for k in (1, 2, 3)]
        buf_a = jnp.zeros((4, 2 * rows, width), view_two.dtype)
        buf_b = jnp.zeros((4, 2 * rows, width), view_two.dtype)
        for k in range(4):
            buf_a = put(buf_a, a[k], (x - k) % 4)
            buf_b = put(buf_b, b[k], (y - k) % 4)
        full = jnp.zeros((4, 4, 2, 2 * rows, width), view_two.dtype)
        for k in range(4):
            got_a = lax.ppermute(buf_a, "y", shift(k)) if k else buf_a
            got_b = lax.ppermute(buf_b, "x", shift(k)) if k else buf_b
            full = lax.dynamic_update_slice(full, got_a[:, None, None], (0, (y - k) % 4, 0, 0, 0))
            full = lax.dynamic_update_slice(full, got_b[None, :, None], ((x - k) % 4, 0, 1, 0, 0))
        second = full.reshape(count, width)
    tile = jnp.stack([x * 4 + y, zh * 4 + slot]).astype(jnp.int32)
    slope, turned, vec = correlate(tile, first, second)
    part_one = back_one(first, second, turned, vec)
    with jax.named_scope("scatter_one"):
        grad_one = lax.psum_scatter(part_one, COLS, tiled=True)
    parts = back_two(jnp.stack([x, y]).astype(jnp.int32), first, second, slope, vec)
    with jax.named_scope("scatter_two"):
        half_a = sum_pieces(parts[:4], "y")
        half_b = sum_pieces(parts[4:], "x")
        half_a = sum_pieces([pick(half_a, (x + k) % 4) for k in range(4)], "x")
        half_b = sum_pieces([pick(half_b, (y + k) % 4) for k in range(4)], "y")
        grad_two = jnp.concatenate([half_a, half_b], 0)
    with jax.named_scope("relayout_back"):
        grad_one = lax.ppermute(grad_one, AXES, turn(True))
        pieces = list(unjoin(q, grad_one, grad_two))
        for k in (1, 2, 3):
            pieces[k] = lax.ppermute(pieces[k], AXES, near(k))
        return tuple(unsplit(q, pieces))


def solution(mesh):
    grid = Mesh(mesh.devices.reshape(SIZES), AXES)
    spread = P(("x", "zl", "y", "c"), "zh")
    return jax.shard_map(
        local, mesh=grid, in_specs=(spread, spread), out_specs=(spread, spread), check_vma=False
    )
```

```python
import functools
import itertools

import jax
import jax.numpy as jnp
from jax import lax
from jax.experimental import pallas as pl
from jax.experimental.pallas import tpu as pltpu
from jax.sharding import Mesh
from jax.sharding import PartitionSpec as P

EPSILON = 1e-05
OFF_WEIGHT = 0.0051
SIZES = (4, 2, 4, 2, 4)
AXES = ("x", "zl", "y", "c", "zh")
COLS = ("zh", "zl", "c")
VMEM = pltpu.VMEM
SMEM = pltpu.SMEM


def device(x, zl, y, c, zh):
    return (((x * 2 + zl) * 4 + y) * 2 + c) * 4 + zh


def near(k):
    out = []
    for x, zl, y, c, zh in itertools.product(*map(range, SIZES)):
        q = (zl * 2 + c) ^ k
        out.append((device(x, zl, y, c, zh), device(x, q // 2, y, q % 2, zh)))
    return out


def shift(k):
    return [(i, (i + k) % 4) for i in range(4)]


def spec(space=VMEM):
    return pl.BlockSpec(memory_space=space)


def split_kernel(q_ref, one, two, blocks, *outs):
    q = q_ref[0]
    width = two.shape[1] // 4
    for k, out in enumerate(outs):
        cols = pl.ds(pl.multiple_of((q ^ k) * width, width), width)
        out[...] = two[:, cols]
    lanes = blocks.shape[2]
    for b in range(16):
        blocks[b] = one[:, b * lanes : (b + 1) * lanes]


def split(q, one, two):
    rows, width = one.shape
    shape = jax.ShapeDtypeStruct((rows, width // 4), one.dtype)
    return pl.pallas_call(
        split_kernel,
        out_shape=[jax.ShapeDtypeStruct((16, rows, width // 16), one.dtype)] + [shape] * 4,
        in_specs=[spec(SMEM), spec(), spec()],
        out_specs=[spec()] * 5,
        name="split",
    )(q, one, two)


def join_kernel(q_ref, p0, p1, p2, p3, two):
    q = q_ref[0]
    for k, piece in enumerate((p0, p1, p2, p3)):
        two[q ^ k] = piece[...]


def join(q, pieces):
    shape = jax.ShapeDtypeStruct((4,) + pieces[0].shape, pieces[0].dtype)
    return pl.pallas_call(
        join_kernel,
        out_shape=shape,
        in_specs=[spec(SMEM)] + [spec()] * 4,
        out_specs=spec(),
        name="join",
    )(q, *pieces)


def unjoin_kernel(q_ref, low, high, *outs):
    q = q_ref[0]
    for k, out in enumerate(outs):
        at = q ^ k

        @pl.when(at < 2)
        def _():
            out[...] = low[at & 1]

        @pl.when(at >= 2)
        def _():
            out[...] = high[at & 1]


def unjoin(q, low, high):
    shape = jax.ShapeDtypeStruct(low.shape[1:], low.dtype)
    return pl.pallas_call(
        unjoin_kernel,
        out_shape=[shape] * 4,
        in_specs=[spec(SMEM), spec(), spec()],
        out_specs=[spec()] * 4,
        name="unjoin",
    )(q, low, high)


def unsplit_two_kernel(q_ref, p0, p1, p2, p3, two):
    q = q_ref[0]
    width = p0.shape[1]
    for k, piece in enumerate((p0, p1, p2, p3)):
        cols = pl.ds(pl.multiple_of((q ^ k) * width, width), width)
        two[:, cols] = piece[...]


def unsplit_two(q, pieces):
    rows, width = pieces[0].shape
    return pl.pallas_call(
        unsplit_two_kernel,
        out_shape=jax.ShapeDtypeStruct((rows, 4 * width), pieces[0].dtype),
        in_specs=[spec(SMEM)] + [spec()] * 4,
        out_specs=spec(),
        name="unsplit_two",
    )(q, *pieces)


def unsplit_one_kernel(blocks, one):
    lanes = blocks.shape[2]
    for b in range(16):
        one[:, b * lanes : (b + 1) * lanes] = blocks[b]


def unsplit_one(blocks):
    _, rows, lanes = blocks.shape
    return pl.pallas_call(
        unsplit_one_kernel,
        out_shape=jax.ShapeDtypeStruct((rows, 16 * lanes), blocks.dtype),
        in_specs=[spec()],
        out_specs=spec(),
        name="unsplit_one",
    )(blocks)


def column(row):
    return jnp.broadcast_to(row, (8, row.shape[1])).T[:, 0:1]


def line(col):
    return jnp.broadcast_to(col, (col.shape[0], 128)).T[0:1, :]


def wide(ref):
    return jnp.concatenate([ref[h] for h in range(4)], 1)


def correlate_kernel(steps, count, tile_ref, one, two, slope_out, turned_out, vec_out, acc, sums):
    step = pl.program_id(0)

    @pl.when(step == 0)
    def _():
        acc[...] = jnp.zeros_like(acc)
        sums[...] = jnp.zeros_like(sums)

    left, right = wide(one), two[...]
    acc[...] += lax.dot_general(
        left, right, (((0,), (0,)), ((), ())), preferred_element_type=jnp.float32
    )
    for at, block in ((0, left), (2, right)):
        value = block.astype(jnp.float32).reshape(block.shape[0] // 8, 8, block.shape[1])
        sums[at] += jnp.sum(value, 0)
        sums[at + 1] += jnp.sum(value * value, 0)

    @pl.when(step == steps - 1)
    def _():
        mean_one = jnp.sum(sums[0], 0, keepdims=True) / count
        mean_two = jnp.sum(sums[2], 0, keepdims=True) / count
        square_one = jnp.sum(sums[1], 0, keepdims=True) / count
        square_two = jnp.sum(sums[3], 0, keepdims=True) / count
        inv_one = lax.rsqrt(square_one - mean_one * mean_one + EPSILON)
        inv_two = lax.rsqrt(square_two - mean_two * mean_two + EPSILON)
        corr = (acc[...] / count - column(mean_one) * mean_two) * (column(inv_one) * inv_two)
        lanes = one.shape[2]
        row = lax.broadcasted_iota(jnp.int32, corr.shape, 0)
        row = (row // lanes) * (16 * lanes) + tile_ref[0] * lanes + row % lanes
        col = lax.broadcasted_iota(jnp.int32, corr.shape, 1) + tile_ref[1] * corr.shape[1]
        slope = jnp.where(row == col, -2.0 * (1.0 - corr), 2.0 * OFF_WEIGHT * corr)
        weight = slope * corr
        proj_one = line(jnp.sum(weight, 1, keepdims=True))
        proj_two = jnp.sum(weight, 0, keepdims=True)
        slope_out[...] = slope.astype(jnp.bfloat16)
        turned_out[...] = slope.T.astype(jnp.bfloat16)
        vec_out[...] = jnp.concatenate(
            [mean_one, inv_one, proj_one, mean_two, inv_two, proj_two, proj_one, proj_two], 0
        )


def correlate(tile, one, two):
    count, width = two.shape
    block = 1024
    steps = count // block
    square = jax.ShapeDtypeStruct((width, width), jnp.bfloat16)
    whole = pl.BlockSpec((width, width), lambda s: (0, 0))
    return pl.pallas_call(
        functools.partial(correlate_kernel, steps, count),
        grid=(steps,),
        out_shape=[square, square, jax.ShapeDtypeStruct((8, width), jnp.float32)],
        in_specs=[
            spec(SMEM),
            pl.BlockSpec((4, block, width // 4), lambda s: (0, s, 0)),
            pl.BlockSpec((block, width), lambda s: (s, 0)),
        ],
        out_specs=[whole, whole, pl.BlockSpec((8, width), lambda s: (0, 0))],
        scratch_shapes=[
            VMEM((width, width), jnp.float32),
            VMEM((4, 8, width), jnp.float32),
        ],
        cost_estimate=pl.CostEstimate(
            flops=2 * count * width * width, bytes_accessed=4 * count * width, transcendentals=0
        ),
        compiler_params=pltpu.CompilerParams(vmem_limit_bytes=40 * 2**20),
        name="correlate",
    )(tile, one, two)


def back(own, other, weight, own_at, other_at, vec):
    mean_own, inv_own, proj_own = (vec[own_at + i : own_at + i + 1, :] for i in range(3))
    mean_other, inv_other = (vec[other_at + i : other_at + i + 1, :] for i in range(2))
    rounded = ((other.astype(jnp.float32) - mean_other) * inv_other).astype(jnp.bfloat16)
    product = jnp.dot(rounded, weight, preferred_element_type=jnp.float32)
    slant = inv_own * inv_own * proj_own
    return (inv_own * product - (own.astype(jnp.float32) - mean_own) * slant).astype(jnp.bfloat16)


def back_one_kernel(one, two, weight, vec, out):
    part = back(wide(one), two[...], weight[...], 0, 3, vec)
    lanes = out.shape[2]
    for h in range(4):
        out[h] = part[:, h * lanes : (h + 1) * lanes]


def back_one(one, two, weight, vec):
    count, width = two.shape
    block = 1024
    columns = pl.BlockSpec((4, block, width // 4), lambda s: (0, s, 0))
    return pl.pallas_call(
        back_one_kernel,
        grid=(count // block,),
        out_shape=jax.ShapeDtypeStruct(one.shape, jnp.bfloat16),
        in_specs=[
            columns,
            pl.BlockSpec((block, width), lambda s: (s, 0)),
            pl.BlockSpec((width, width), lambda s: (0, 0)),
            pl.BlockSpec((8, width), lambda s: (0, 0)),
        ],
        out_specs=columns,
        cost_estimate=pl.CostEstimate(
            flops=2 * count * width * width, bytes_accessed=6 * count * width, transcendentals=0
        ),
        compiler_params=pltpu.CompilerParams(vmem_limit_bytes=40 * 2**20),
        name="back_one",
    )(one, two, weight, vec)


def back_two_kernel(pos, one, two, weight, vec, out):
    for h in range(2):
        out[h, 0] = back(two[h, 0], wide(one.at[:, h, 0]), weight[...], 3, 0, vec)


def back_two(pos, one, two, weight, vec, half, k):
    _, _, rows, width = two.shape

    def block(t, pos):
        if half == 0:
            return t * 4 + (pos[1] + k) % 4
        return ((pos[0] + k) % 4) * 4 + t

    return pl.pallas_call(
        back_two_kernel,
        grid_spec=pltpu.PrefetchScalarGridSpec(
            num_scalar_prefetch=1,
            grid=(4,),
            in_specs=[
                pl.BlockSpec(
                    (4, 2, 1, rows, width // 4), lambda t, pos: (0, half, block(t, pos), 0, 0)
                ),
                pl.BlockSpec((2, 1, rows, width), lambda t, pos: (half, block(t, pos), 0, 0)),
                pl.BlockSpec((width, width), lambda t, pos: (0, 0)),
                pl.BlockSpec((8, width), lambda t, pos: (0, 0)),
            ],
            out_specs=pl.BlockSpec((2, 1, rows, width), lambda t, pos: (0, t, 0, 0)),
        ),
        out_shape=jax.ShapeDtypeStruct((2, 4, rows, width), jnp.bfloat16),
        cost_estimate=pl.CostEstimate(
            flops=16 * rows * width * width, bytes_accessed=48 * rows * width, transcendentals=0
        ),
        compiler_params=pltpu.CompilerParams(vmem_limit_bytes=40 * 2**20),
        name="back_two",
    )(pos, one, two, weight, vec)


def sum_pieces(pieces, axis):
    total = pieces[0].astype(jnp.float32)
    for k in (1, 2, 3):
        total += lax.ppermute(pieces[k], axis, shift(k)).astype(jnp.float32)
    return total.astype(jnp.bfloat16)


def pick(blocks, index):
    return lax.dynamic_index_in_dim(blocks, index, 1, keepdims=False)


def put(buffer, piece, index):
    return lax.dynamic_update_index_in_dim(buffer, piece, index, 1)


def local(view_one, view_two):
    x, y = lax.axis_index("x"), lax.axis_index("y")
    zl, c, zh = lax.axis_index("zl"), lax.axis_index("c"), lax.axis_index("zh")
    slot = zl * 2 + c
    q = slot.astype(jnp.int32).reshape(1)
    pos = jnp.stack([x, y]).astype(jnp.int32)
    rows = view_one.shape[0]
    width = view_one.shape[1] // 4
    lanes = width // 4
    count = rows * 64
    with jax.named_scope("relayout"):
        blocks, *pieces = split(q, view_one, view_two)
        for k in (1, 2, 3):
            pieces[k] = lax.ppermute(pieces[k], AXES, near(k))
        own_one = lax.all_to_all(blocks, ("x", "y"), 0, 0, tiled=True)
        own_two = join(q, pieces)
    with jax.named_scope("gather_one"):
        first = lax.all_gather(own_one.reshape(16 * rows, lanes), COLS, tiled=True)
    with jax.named_scope("gather_two"):
        low, high = own_two[:2], own_two[2:]
        a = [low] + [lax.ppermute(low, "x", shift(k)) for k in (1, 2, 3)]
        b = [high] + [lax.ppermute(high, "y", shift(k)) for k in (1, 2, 3)]
        buf_a = jnp.zeros((2, 4, rows, width), view_two.dtype)
        buf_b = jnp.zeros((2, 4, rows, width), view_two.dtype)
        for k in range(4):
            buf_a = put(buf_a, a[k], (x - k) % 4)
            buf_b = put(buf_b, b[k], (y - k) % 4)
        full = jnp.zeros((4, 4, 4, rows, width), view_two.dtype)
        for k in range(4):
            got_a = lax.ppermute(buf_a, "y", shift(k)) if k else buf_a
            got_b = lax.ppermute(buf_b, "x", shift(k)) if k else buf_b
            full = lax.dynamic_update_slice(full, got_a[:, :, None], (0, 0, (y - k) % 4, 0, 0))
            full = lax.dynamic_update_slice(full, got_b[:, None], (2, (x - k) % 4, 0, 0, 0))
        second = full.reshape(count, width)
    tile = jnp.stack([x * 4 + y, zh * 4 + slot]).astype(jnp.int32)
    slope, turned, vec = correlate(tile, first.reshape(4, count, lanes), second)
    part_one = back_one(first.reshape(4, count, lanes), second, turned, vec)
    with jax.named_scope("scatter_one"):
        grad_one = lax.psum_scatter(part_one.reshape(4 * count, lanes), COLS, tiled=True)
    first = first.reshape(4, 4, 16, rows, lanes)
    second = second.reshape(4, 16, rows, width)
    with jax.named_scope("scatter_two"):
        low = [back_two(pos, first, second, slope, vec, 0, k) for k in range(4)]
        high = [back_two(pos, first, second, slope, vec, 1, k) for k in range(4)]
        low = sum_pieces(low, "y")
        high = sum_pieces(high, "x")
        low = sum_pieces([pick(low, (x + k) % 4) for k in range(4)], "x")
        high = sum_pieces([pick(high, (y + k) % 4) for k in range(4)], "y")
    with jax.named_scope("relayout_back"):
        pieces = list(unjoin(q, low, high))
        for k in (1, 2, 3):
            pieces[k] = lax.ppermute(pieces[k], AXES, near(k))
        grad_two = unsplit_two(q, pieces)
        grad_one = lax.all_to_all(grad_one.reshape(16, rows, lanes), ("x", "y"), 0, 0, tiled=True)
        return unsplit_one(grad_one), grad_two


def solution(mesh):
    grid = Mesh(mesh.devices.reshape(SIZES), AXES)
    spread = P(("x", "zl", "y", "c"), "zh")
    return jax.shard_map(
        local, mesh=grid, in_specs=(spread, spread), out_specs=(spread, spread), check_vma=False
    )
```

```python
import functools
import itertools

import jax
import jax.numpy as jnp
from jax import lax
from jax.experimental import pallas as pl
from jax.experimental.pallas import tpu as pltpu
from jax.sharding import Mesh
from jax.sharding import PartitionSpec as P

EPSILON = 1e-05
OFF_WEIGHT = 0.0051
SIZES = (4, 2, 4, 2, 4)
AXES = ("x", "zl", "y", "c", "zh")
COLS = ("zh", "zl", "c")
VMEM = pltpu.VMEM
SMEM = pltpu.SMEM


def device(x, zl, y, c, zh):
    return (((x * 2 + zl) * 4 + y) * 2 + c) * 4 + zh


def near(k):
    out = []
    for x, zl, y, c, zh in itertools.product(*map(range, SIZES)):
        q = (zl * 2 + c) ^ k
        out.append((device(x, zl, y, c, zh), device(x, q // 2, y, q % 2, zh)))
    return out


def shift(k):
    return [(i, (i + k) % 4) for i in range(4)]


def spec(space=VMEM):
    return pl.BlockSpec(memory_space=space)


def split_kernel(q_ref, one, two, blocks, *outs):
    q = q_ref[0]
    width = two.shape[1] // 4
    for k, out in enumerate(outs):
        cols = pl.ds(pl.multiple_of((q ^ k) * width, width), width)
        out[...] = two[:, cols]
    lanes = blocks.shape[2]
    for b in range(16):
        blocks[b] = one[:, b * lanes : (b + 1) * lanes]


def split(q, one, two):
    rows, width = one.shape
    shape = jax.ShapeDtypeStruct((rows, width // 4), one.dtype)
    return pl.pallas_call(
        split_kernel,
        out_shape=[jax.ShapeDtypeStruct((16, rows, width // 16), one.dtype)] + [shape] * 4,
        in_specs=[spec(SMEM), spec(), spec()],
        out_specs=[spec()] * 5,
        name="split",
    )(q, one, two)


def join_kernel(q_ref, p0, p1, p2, p3, two):
    q = q_ref[0]
    for k, piece in enumerate((p0, p1, p2, p3)):
        two[q ^ k] = piece[...]


def join(q, pieces):
    shape = jax.ShapeDtypeStruct((4,) + pieces[0].shape, pieces[0].dtype)
    return pl.pallas_call(
        join_kernel,
        out_shape=shape,
        in_specs=[spec(SMEM)] + [spec()] * 4,
        out_specs=spec(),
        name="join",
    )(q, *pieces)


def unjoin_kernel(q_ref, low, high, *outs):
    q = q_ref[0]
    for k, out in enumerate(outs):
        at = q ^ k

        @pl.when(at < 2)
        def _():
            out[...] = low[at & 1]

        @pl.when(at >= 2)
        def _():
            out[...] = high[at & 1]


def unjoin(q, low, high):
    shape = jax.ShapeDtypeStruct(low.shape[1:], low.dtype)
    return pl.pallas_call(
        unjoin_kernel,
        out_shape=[shape] * 4,
        in_specs=[spec(SMEM), spec(), spec()],
        out_specs=[spec()] * 4,
        name="unjoin",
    )(q, low, high)


def unsplit_two_kernel(q_ref, p0, p1, p2, p3, two):
    q = q_ref[0]
    width = p0.shape[1]
    for k, piece in enumerate((p0, p1, p2, p3)):
        cols = pl.ds(pl.multiple_of((q ^ k) * width, width), width)
        two[:, cols] = piece[...]


def unsplit_two(q, pieces):
    rows, width = pieces[0].shape
    return pl.pallas_call(
        unsplit_two_kernel,
        out_shape=jax.ShapeDtypeStruct((rows, 4 * width), pieces[0].dtype),
        in_specs=[spec(SMEM)] + [spec()] * 4,
        out_specs=spec(),
        name="unsplit_two",
    )(q, *pieces)


def unsplit_one_kernel(blocks, one):
    lanes = blocks.shape[2]
    for b in range(16):
        one[:, b * lanes : (b + 1) * lanes] = blocks[b]


def unsplit_one(blocks):
    _, rows, lanes = blocks.shape
    return pl.pallas_call(
        unsplit_one_kernel,
        out_shape=jax.ShapeDtypeStruct((rows, 16 * lanes), blocks.dtype),
        in_specs=[spec()],
        out_specs=spec(),
        name="unsplit_one",
    )(blocks)


def column(row):
    return jnp.broadcast_to(row, (8, row.shape[1])).T[:, 0:1]


def line(col):
    return jnp.broadcast_to(col, (col.shape[0], 128)).T[0:1, :]


def wide(ref):
    return jnp.concatenate([ref[h].reshape(-1, ref.shape[-1]) for h in range(4)], 1)


def gather_block(pos, pieces, held):
    step = pl.program_id(0)
    low, high = pieces[:8], pieces[8:]
    for k in range(4):

        @pl.when(step // 2 == k)
        def _():
            held[0:1] = low[2 * k][...]
            held[1:2] = low[2 * k + 1][...]

    for u in range(2):
        turn = (pos[0] - (step % 2) * 2 - u) % 4
        for k in range(4):

            @pl.when(turn == k)
            def _():
                held[2, u] = high[2 * k][0, 0]
                held[3, u] = high[2 * k + 1][0, 0]


def block_specs(rows, lanes, pieces):
    def ones(s, pos):
        return (0, 0, s % 2, (pos[1] - s // 2) % 4, 0, 0)

    def low(k, part):
        return lambda s, pos: (part, jnp.clip(s - 2 * k, 0, 1), 0, 0)

    def high(part):
        return lambda s, pos: (part, (pos[1] - s // 2) % 4, 0, 0)

    one = pl.BlockSpec((4, 4, 2, 1, rows, lanes), ones)
    twos = [
        pl.BlockSpec((1, 2, rows, 4 * lanes), low(k, piece[1]))
        for k in range(4)
        for piece in pieces[k]
    ]
    twos += [
        pl.BlockSpec((1, 1, rows, 4 * lanes), high(piece[1]))
        for k in range(4)
        for piece in pieces[4 + k]
    ]
    return one, twos, [piece[0] for pair in pieces for piece in pair]


def correlate_kernel(count, pos, one, *refs):
    pieces, (slope_out, turned_out, vec_out, acc, sums, held) = refs[:16], refs[16:]
    step = pl.program_id(0)

    @pl.when(step == 0)
    def _():
        acc[...] = jnp.zeros_like(acc)
        sums[...] = jnp.zeros_like(sums)

    gather_block(pos, pieces, held)
    left, right = wide(one), held[...].reshape(-1, held.shape[-1])
    acc[...] += lax.dot_general(
        left, right, (((0,), (0,)), ((), ())), preferred_element_type=jnp.float32
    )
    for at, block in ((0, left), (2, right)):
        value = block.astype(jnp.float32).reshape(block.shape[0] // 8, 8, block.shape[1])
        sums[at] += jnp.sum(value, 0)
        sums[at + 1] += jnp.sum(value * value, 0)

    @pl.when(step == 7)
    def _():
        mean_one = jnp.sum(sums[0], 0, keepdims=True) / count
        mean_two = jnp.sum(sums[2], 0, keepdims=True) / count
        square_one = jnp.sum(sums[1], 0, keepdims=True) / count
        square_two = jnp.sum(sums[3], 0, keepdims=True) / count
        inv_one = lax.rsqrt(square_one - mean_one * mean_one + EPSILON)
        inv_two = lax.rsqrt(square_two - mean_two * mean_two + EPSILON)
        corr = (acc[...] / count - column(mean_one) * mean_two) * (column(inv_one) * inv_two)
        lanes = one.shape[-1]
        row = lax.broadcasted_iota(jnp.int32, corr.shape, 0)
        row = (row // lanes) * (16 * lanes) + (pos[0] * 4 + pos[1]) * lanes + row % lanes
        col = lax.broadcasted_iota(jnp.int32, corr.shape, 1) + pos[2] * corr.shape[1]
        slope = jnp.where(row == col, -2.0 * (1.0 - corr), 2.0 * OFF_WEIGHT * corr)
        weight = slope * corr
        proj_one = line(jnp.sum(weight, 1, keepdims=True))
        proj_two = jnp.sum(weight, 0, keepdims=True)
        slope_out[...] = slope.astype(jnp.bfloat16)
        turned_out[...] = slope.T.astype(jnp.bfloat16)
        vec_out[...] = jnp.concatenate(
            [mean_one, inv_one, proj_one, mean_two, inv_two, proj_two, proj_one, proj_two], 0
        )


def correlate(pos, one, pieces):
    rows, lanes = one.shape[4:]
    width = 4 * lanes
    count = 64 * rows
    square = jax.ShapeDtypeStruct((width, width), jnp.bfloat16)
    whole = pl.BlockSpec((width, width), lambda s, pos: (0, 0))
    first, seconds, arrays = block_specs(rows, lanes, pieces)
    return pl.pallas_call(
        functools.partial(correlate_kernel, count),
        grid_spec=pltpu.PrefetchScalarGridSpec(
            num_scalar_prefetch=1,
            grid=(8,),
            in_specs=[first] + seconds,
            out_specs=[whole, whole, pl.BlockSpec((8, width), lambda s, pos: (0, 0))],
            scratch_shapes=[
                VMEM((width, width), jnp.float32),
                VMEM((4, 8, width), jnp.float32),
                VMEM((4, 2, rows, width), jnp.bfloat16),
            ],
        ),
        out_shape=[square, square, jax.ShapeDtypeStruct((8, width), jnp.float32)],
        cost_estimate=pl.CostEstimate(
            flops=2 * count * width * width, bytes_accessed=4 * count * width, transcendentals=0
        ),
        compiler_params=pltpu.CompilerParams(vmem_limit_bytes=40 * 2**20),
        name="correlate",
    )(pos, one, *arrays)


def back(own, other, weight, own_at, other_at, vec):
    mean_own, inv_own, proj_own = (vec[own_at + i : own_at + i + 1, :] for i in range(3))
    mean_other, inv_other = (vec[other_at + i : other_at + i + 1, :] for i in range(2))
    rounded = ((other.astype(jnp.float32) - mean_other) * inv_other).astype(jnp.bfloat16)
    product = jnp.dot(rounded, weight, preferred_element_type=jnp.float32)
    slant = inv_own * inv_own * proj_own
    return (inv_own * product - (own.astype(jnp.float32) - mean_own) * slant).astype(jnp.bfloat16)


def back_one_kernel(pos, one, *refs):
    pieces, (weight, vec, out, held) = refs[:16], refs[16:]
    gather_block(pos, pieces, held)
    part = back(wide(one), held[...].reshape(-1, held.shape[-1]), weight[...], 0, 3, vec)
    lanes = out.shape[-1]
    for h in range(4):
        out[h] = part[:, h * lanes : (h + 1) * lanes].reshape(out.shape[1:])


def back_one(pos, one, pieces, weight, vec):
    rows, lanes = one.shape[4:]
    width = 4 * lanes
    count = 64 * rows
    first, seconds, arrays = block_specs(rows, lanes, pieces)
    return pl.pallas_call(
        back_one_kernel,
        grid_spec=pltpu.PrefetchScalarGridSpec(
            num_scalar_prefetch=1,
            grid=(8,),
            in_specs=[first]
            + seconds
            + [
                pl.BlockSpec((width, width), lambda s, pos: (0, 0)),
                pl.BlockSpec((8, width), lambda s, pos: (0, 0)),
            ],
            out_specs=first,
            scratch_shapes=[VMEM((4, 2, rows, width), jnp.bfloat16)],
        ),
        out_shape=jax.ShapeDtypeStruct(one.shape, jnp.bfloat16),
        cost_estimate=pl.CostEstimate(
            flops=2 * count * width * width, bytes_accessed=6 * count * width, transcendentals=0
        ),
        compiler_params=pltpu.CompilerParams(vmem_limit_bytes=40 * 2**20),
        name="back_one",
    )(pos, one, *arrays, weight, vec)


def back_two_kernel(k, pos, *refs):
    one_low, one_high = refs[:2]
    twos, (weight, vec), refs = refs[2:6], refs[6:8], refs[8:]
    extras, outs = (refs[:2], refs[2:]) if k in (1, 3) else ((None, None), refs)
    for at, (one, extra) in enumerate(((one_low, extras[0]), (one_high, extras[1]))):
        for part in range(2):
            own = twos[2 * at + part]
            other = wide(one.at[:, part])
            value = back(own[...].reshape(-1, own.shape[-1]), other, weight[...], 3, 0, vec)
            value = value.reshape(own.shape[1:])
            if extra is not None and part == (0 if k == 1 else 1):
                value = value.astype(jnp.float32) + extra[0].astype(jnp.float32)
                value = value.astype(jnp.bfloat16)
            if k == 2:
                outs[2 * at + part][0] = value
            else:
                outs[at][part] = value


def back_two(pos, one, pieces, weight, vec, k, extras=()):
    rows, lanes = one.shape[4:]
    width = 4 * lanes
    mine = pieces[-k % 4] + pieces[4 + -k % 4]

    def part(at):
        return pl.BlockSpec((1, 2, rows, width), lambda t, pos: (at, t, 0, 0))

    if k == 2:
        outs, shape = [part(0)] * 4, jax.ShapeDtypeStruct((1, 4, rows, width), jnp.bfloat16)
    else:
        outs = [pl.BlockSpec((2, 2, rows, width), lambda t, pos: (0, t, 0, 0))] * 2
        shape = jax.ShapeDtypeStruct((2, 4, rows, width), jnp.bfloat16)
    return pl.pallas_call(
        functools.partial(back_two_kernel, k),
        grid_spec=pltpu.PrefetchScalarGridSpec(
            num_scalar_prefetch=1,
            grid=(2,),
            in_specs=[
                pl.BlockSpec(
                    (4, 2, 2, 1, rows, lanes), lambda t, pos: (0, 0, t, (pos[1] + k) % 4, 0, 0)
                ),
                pl.BlockSpec(
                    (4, 2, 1, 2, rows, lanes), lambda t, pos: (0, 1, (pos[0] + k) % 4, t, 0, 0)
                ),
            ]
            + [part(piece[1]) for piece in mine]
            + [
                pl.BlockSpec((width, width), lambda t, pos: (0, 0)),
                pl.BlockSpec((8, width), lambda t, pos: (0, 0)),
            ]
            + [part(0) for _ in extras],
            out_specs=outs,
        ),
        out_shape=[shape] * len(outs),
        cost_estimate=pl.CostEstimate(
            flops=32 * rows * width * width, bytes_accessed=96 * rows * width, transcendentals=0
        ),
        compiler_params=pltpu.CompilerParams(vmem_limit_bytes=40 * 2**20),
        name="back_two",
    )(pos, one, one, *[piece[0] for piece in mine], weight, vec, *extras)


def gather_ring(value, axis):
    behind = lax.ppermute(value, axis, shift(1))
    ahead = lax.ppermute(value, axis, shift(3))
    far = [
        lax.ppermute(behind[0:1], axis, shift(1)),
        lax.ppermute(ahead[1:2], axis, shift(3)),
    ]
    return [[(value, 0), (value, 1)], [(behind, 0), (behind, 1)], [(far[0], 0), (far[1], 0)]] + [
        [(ahead, 0), (ahead, 1)]
    ]


def sum_pieces(pieces, axis):
    total = pieces[0].astype(jnp.float32)
    for k in (1, 3, 2):
        total += lax.ppermute(pieces[k], axis, shift(k)).astype(jnp.float32)
    return total.astype(jnp.bfloat16)


def pick(blocks, index):
    return lax.dynamic_index_in_dim(blocks, index, 1, keepdims=False)


def put(buffer, piece, index):
    return lax.dynamic_update_index_in_dim(buffer, piece, index, 1)


def local(view_one, view_two):
    x, y = lax.axis_index("x"), lax.axis_index("y")
    zl, c, zh = lax.axis_index("zl"), lax.axis_index("c"), lax.axis_index("zh")
    slot = zl * 2 + c
    q = slot.astype(jnp.int32).reshape(1)
    pos = jnp.stack([x, y, zh * 4 + slot]).astype(jnp.int32)
    rows = view_one.shape[0]
    width = view_one.shape[1] // 4
    lanes = width // 4
    with jax.named_scope("relayout"):
        blocks, *pieces = split(q, view_one, view_two)
        for k in (1, 2, 3):
            pieces[k] = lax.ppermute(pieces[k], AXES, near(k))
        own_one = lax.all_to_all(blocks, ("x", "y"), 0, 0, tiled=True)
        own_two = join(q, pieces)
        own_one, own_two = lax.optimization_barrier((own_one, own_two))
    with jax.named_scope("gather_one"):
        first = lax.all_gather(own_one.reshape(16 * rows, lanes), COLS, tiled=True)
    with jax.named_scope("gather_two"):
        a, b = own_two[:2], own_two[2:]
        low = jnp.zeros((2, 4, rows, width), view_two.dtype)
        high = jnp.zeros((2, 4, rows, width), view_two.dtype)
        for k in (0, 1, 3, 2):
            low = put(low, lax.ppermute(a, "x", shift(k)) if k else a, (x - k) % 4)
            high = put(high, lax.ppermute(b, "y", shift(k)) if k else b, (y - k) % 4)
        low, high = lax.optimization_barrier((low, high))
        gathered = gather_ring(low, "y") + gather_ring(high, "x")
    first = first.reshape(4, 4, 4, 4, rows, lanes)
    slope, turned, vec = correlate(pos, first, gathered)
    part_one = back_one(pos, first, gathered, turned, vec)
    with jax.named_scope("scatter_one"):
        grad_one = lax.psum_scatter(part_one.reshape(256 * rows, lanes), COLS, tiled=True)
    with jax.named_scope("scatter_two"):
        far = back_two(pos, first, gathered, slope, vec, 2)
        behind = [lax.ppermute(far[at], axis, shift(1)) for at, axis in ((0, "y"), (2, "x"))]
        ahead = [lax.ppermute(far[at], axis, shift(3)) for at, axis in ((1, "y"), (3, "x"))]
        own = back_two(pos, first, gathered, slope, vec, 0)
        up = back_two(pos, first, gathered, slope, vec, 1, behind)
        down = back_two(pos, first, gathered, slope, vec, 3, ahead)
        low, high = (
            (
                own[at].astype(jnp.float32)
                + lax.ppermute(up[at], axis, shift(1)).astype(jnp.float32)
                + lax.ppermute(down[at], axis, shift(3)).astype(jnp.float32)
            ).astype(jnp.bfloat16)
            for at, axis in ((0, "y"), (1, "x"))
        )
        low = sum_pieces([pick(low, (x + k) % 4) for k in range(4)], "x")
        high = sum_pieces([pick(high, (y + k) % 4) for k in range(4)], "y")
    with jax.named_scope("relayout_back"):
        pieces = list(unjoin(q, low, high))
        for k in (1, 2, 3):
            pieces[k] = lax.ppermute(pieces[k], AXES, near(k))
        grad_two = unsplit_two(q, pieces)
        grad_one = lax.all_to_all(grad_one.reshape(16, rows, lanes), ("x", "y"), 0, 0, tiled=True)
        return unsplit_one(grad_one), grad_two


def solution(mesh):
    grid = Mesh(mesh.devices.reshape(SIZES), AXES)
    spread = P(("x", "zl", "y", "c"), "zh")
    return jax.shard_map(
        local, mesh=grid, in_specs=(spread, spread), out_specs=(spread, spread), check_vma=False
    )
```

```python
import functools
import itertools

import jax
import jax.numpy as jnp
from jax import lax
from jax.experimental import pallas as pl
from jax.experimental.pallas import tpu as pltpu
from jax.sharding import Mesh
from jax.sharding import PartitionSpec as P

EPSILON = 1e-05
OFF_WEIGHT = 0.0051
SIZES = (4, 2, 4, 2, 4)
AXES = ("x", "zl", "y", "c", "zh")
COLS = ("zh", "zl", "c")
VMEM = pltpu.VMEM
LIMIT = 58 * 2**20
SMEM = pltpu.SMEM


def device(x, zl, y, c, zh):
    return (((x * 2 + zl) * 4 + y) * 2 + c) * 4 + zh


def near(k):
    out = []
    for x, zl, y, c, zh in itertools.product(*map(range, SIZES)):
        q = (zl * 2 + c) ^ k
        out.append((device(x, zl, y, c, zh), device(x, q // 2, y, q % 2, zh)))
    return out


def shift(k):
    return [(i, (i + k) % 4) for i in range(4)]


def spec(space=VMEM):
    return pl.BlockSpec(memory_space=space)


def split_kernel(q_ref, one, two, blocks, *outs):
    q = q_ref[0]
    width = two.shape[1] // 4
    for k, out in enumerate(outs):
        cols = pl.ds(pl.multiple_of((q ^ k) * width, width), width)
        out[...] = two[:, cols]
    lanes = blocks.shape[2]
    for b in range(16):
        blocks[b] = one[:, b * lanes : (b + 1) * lanes]


def split(q, one, two):
    rows, width = one.shape
    shape = jax.ShapeDtypeStruct((rows, width // 4), one.dtype)
    return pl.pallas_call(
        split_kernel,
        out_shape=[jax.ShapeDtypeStruct((16, rows, width // 16), one.dtype)] + [shape] * 4,
        in_specs=[spec(SMEM), spec(), spec()],
        out_specs=[spec()] * 5,
        name="split",
    )(q, one, two)


def join_kernel(q_ref, p0, p1, p2, p3, low, high):
    q = q_ref[0]
    for k, piece in enumerate((p0, p1, p2, p3)):
        at = q ^ k

        @pl.when(at < 2)
        def _():
            low[at & 1] = piece[...]

        @pl.when(at >= 2)
        def _():
            high[at & 1] = piece[...]


def join(q, pieces):
    shape = jax.ShapeDtypeStruct((2,) + pieces[0].shape, pieces[0].dtype)
    return pl.pallas_call(
        join_kernel,
        out_shape=[shape] * 2,
        in_specs=[spec(SMEM)] + [spec()] * 4,
        out_specs=[spec()] * 2,
        name="join",
    )(q, *pieces)


def total(*refs):
    return functools.reduce(jnp.add, [ref.astype(jnp.float32) for ref in refs]).astype(jnp.bfloat16)


def sum_pick_kernel(me, *refs):
    for k, out in enumerate(refs[6:]):
        at = (me[0] + k) % 4
        out[0] = total(*[ref[0, at] for ref in refs[:3]])
        out[1] = total(*[ref[0, at] for ref in refs[3:6]])


def sum_pick(me, terms):
    _, _, rows, width = terms[0].shape
    return pl.pallas_call(
        sum_pick_kernel,
        out_shape=[jax.ShapeDtypeStruct((2, rows, width), jnp.bfloat16)] * 4,
        in_specs=[spec(SMEM)] + [spec()] * 6,
        out_specs=[spec()] * 4,
        name="sum_pick",
    )(me, *terms)


def unjoin_kernel(q_ref, *refs):
    q = q_ref[0]
    low, high, outs = refs[:4], refs[4:8], refs[8:]
    for k, out in enumerate(outs):
        at = q ^ k

        @pl.when(at < 2)
        def _():
            out[...] = total(*[ref[at & 1] for ref in low])

        @pl.when(at >= 2)
        def _():
            out[...] = total(*[ref[at & 1] for ref in high])


def unjoin(q, low, high):
    return pl.pallas_call(
        unjoin_kernel,
        out_shape=[jax.ShapeDtypeStruct(low[0].shape[1:], jnp.bfloat16)] * 4,
        in_specs=[spec(SMEM)] + [spec()] * 8,
        out_specs=[spec()] * 4,
        name="unjoin",
    )(q, *low, *high)


def unsplit_kernel(q_ref, blocks, p0, p1, p2, p3, one, two):
    q = q_ref[0]
    width = p0.shape[1]
    for k, piece in enumerate((p0, p1, p2, p3)):
        cols = pl.ds(pl.multiple_of((q ^ k) * width, width), width)
        two[:, cols] = piece[...]
    lanes = blocks.shape[2]
    for b in range(16):
        one[:, b * lanes : (b + 1) * lanes] = blocks[b]


def unsplit(q, blocks, pieces):
    rows, width = pieces[0].shape
    shape = jax.ShapeDtypeStruct((rows, 4 * width), pieces[0].dtype)
    return pl.pallas_call(
        unsplit_kernel,
        out_shape=[shape] * 2,
        in_specs=[spec(SMEM)] + [spec()] * 5,
        out_specs=[spec()] * 2,
        name="unsplit",
    )(q, blocks, *pieces)


def column(row):
    return jnp.broadcast_to(row, (8, row.shape[1])).T[:, 0:1]


def line(col):
    return jnp.broadcast_to(col, (col.shape[0], 128)).T[0:1, :]


def chunk(buffer, *at):
    blocks = [buffer[(h,) + at] for h in range(4)]
    return jnp.concatenate([block.reshape(-1, block.shape[-1]) for block in blocks], 1)


def back(own, other, weight, own_at, other_at, vec):
    mean_own, inv_own, proj_own = (vec[own_at + i : own_at + i + 1, :] for i in range(3))
    mean_other, inv_other = (vec[other_at + i : other_at + i + 1, :] for i in range(2))
    rounded = ((other.astype(jnp.float32) - mean_other) * inv_other).astype(jnp.bfloat16)
    product = jnp.dot(rounded, weight, preferred_element_type=jnp.float32)
    slant = inv_own * inv_own * proj_own
    return (inv_own * product - (own.astype(jnp.float32) - mean_own) * slant).astype(jnp.bfloat16)


def finish(count, pos, acc, sums, lanes):
    mean_one = jnp.sum(sums[0], 0, keepdims=True) / count
    mean_two = jnp.sum(sums[2], 0, keepdims=True) / count
    square_one = jnp.sum(sums[1], 0, keepdims=True) / count
    square_two = jnp.sum(sums[3], 0, keepdims=True) / count
    inv_one = lax.rsqrt(square_one - mean_one * mean_one + EPSILON)
    inv_two = lax.rsqrt(square_two - mean_two * mean_two + EPSILON)
    corr = (acc[...] / count - column(mean_one) * mean_two) * (column(inv_one) * inv_two)
    row = lax.broadcasted_iota(jnp.int32, corr.shape, 0)
    row = (row // lanes) * (16 * lanes) + (pos[0] * 4 + pos[1]) * lanes + row % lanes
    col = lax.broadcasted_iota(jnp.int32, corr.shape, 1) + pos[2] * corr.shape[1]
    slope = jnp.where(row == col, -2.0 * (1.0 - corr), 2.0 * OFF_WEIGHT * corr)
    weight = slope * corr
    proj_one = line(jnp.sum(weight, 1, keepdims=True))
    proj_two = jnp.sum(weight, 0, keepdims=True)
    rows = [mean_one, inv_one, proj_one, mean_two, inv_two, proj_two, proj_one, proj_two]
    return slope, jnp.concatenate(rows, 0)


def tile_kernel(count, places, pos, one, *refs):
    arrays, refs = refs[: len(places)], refs[len(places) :]
    part_out, slope_out, vec_out, buf_one, buf_two, acc, sums, turned, parts, in_sem, out_sem = refs
    lanes = one.shape[-1]
    loads = [[], [], [], []]
    for q in range(4):
        for h in range(4):
            loads[q].append((one.at[h, q], buf_one.at[h, q]))
    for ref, place in zip(arrays, places):
        q, k, index = place
        if q < 2:
            target = buf_two.at[q, :, (pos[1] - k) % 4]
        else:
            target = buf_two.at[q, (pos[0] - k) % 4]
        loads[q].append((ref.at[index], target))
    loads = [
        [pltpu.make_async_copy(src, dst, in_sem.at[q, i]) for i, (src, dst) in enumerate(row)]
        for q, row in enumerate(loads)
    ]
    for row in loads:
        for copy in row:
            copy.start()
    acc[...] = jnp.zeros_like(acc)
    sums[...] = jnp.zeros_like(sums)
    for q in range(4):
        for copy in loads[q]:
            copy.wait()

        @pl.loop(0, 4)
        def _(y):
            left = chunk(buf_one, q, slice(None), y)
            right = buf_two[q, :, y].reshape(left.shape)
            acc[...] += lax.dot_general(
                left, right, (((0,), (0,)), ((), ())), preferred_element_type=jnp.float32
            )
            for at, block in ((0, left), (2, right)):
                value = block.astype(jnp.float32).reshape(block.shape[0] // 8, 8, block.shape[1])
                sums[at] += jnp.sum(value, 0)
                sums[at + 1] += jnp.sum(value * value, 0)

    slope, vec = finish(count, pos, acc, sums, lanes)
    slope_out[...] = slope.astype(jnp.bfloat16)
    turned[...] = slope.T.astype(jnp.bfloat16)
    vec_out[...] = vec

    def write(step, h):
        rows = part_out.at[h, step // 4, :, step % 4]
        return pltpu.make_async_copy(parts.at[step % 4, h], rows, out_sem.at[step % 4, h])

    @pl.loop(0, 16)
    def _(step):
        @pl.when(step >= 4)
        def _():
            for h in range(4):
                write(step - 4, h).wait()

        q, y = step // 4, step % 4
        own = chunk(buf_one, q, slice(None), y)
        other = buf_two[q, :, y].reshape(own.shape)
        part = back(own, other, turned[...], 0, 3, vec_out)
        for h in range(4):
            block = part[:, h * lanes : (h + 1) * lanes]
            parts[step % 4, h] = block.reshape(parts.shape[2:])
            write(step, h).start()

    for step in range(12, 16):
        for h in range(4):
            write(step, h).wait()


def tile_work(pos, one, pieces):
    rows, lanes = one.shape[4:]
    width = 4 * lanes
    count = 64 * rows
    arrays, places = [], []
    for at in range(8):
        for part in range(2):
            array, index = pieces[at][part]
            arrays.append(array)
            places.append((2 * (at // 4) + part, at % 4, index))
    anywhere = pl.BlockSpec(memory_space=pl.ANY)
    return pl.pallas_call(
        functools.partial(tile_kernel, count, places),
        in_specs=[spec(SMEM)] + [anywhere] * 17,
        out_specs=[anywhere, spec(), spec()],
        out_shape=[
            jax.ShapeDtypeStruct(one.shape, jnp.bfloat16),
            jax.ShapeDtypeStruct((width, width), jnp.bfloat16),
            jax.ShapeDtypeStruct((8, width), jnp.float32),
        ],
        scratch_shapes=[
            VMEM((4, 4, 4, 4, rows, lanes), jnp.bfloat16),
            VMEM((4, 4, 4, rows, width), jnp.bfloat16),
            VMEM((width, width), jnp.float32),
            VMEM((4, 8, width), jnp.float32),
            VMEM((width, width), jnp.bfloat16),
            VMEM((4, 4, 4, rows, lanes), jnp.bfloat16),
            pltpu.SemaphoreType.DMA((4, 8)),
            pltpu.SemaphoreType.DMA((4, 4)),
        ],
        cost_estimate=pl.CostEstimate(
            flops=4 * count * width * width, bytes_accessed=6 * count * width, transcendentals=0
        ),
        compiler_params=pltpu.CompilerParams(vmem_limit_bytes=LIMIT),
        name="tile",
    )(pos, one, *arrays)


def back_two_kernel(items, indices, pos, one, *refs):
    count = len(items)
    arrays, (weight, vec), refs = refs[:count], refs[count : count + 2], refs[count + 2 :]
    extras, outs, scratch = refs[: -count - 6], refs[-count - 6 : -6], refs[-6:]
    buf_one, buf_two, buf_extra, parts, in_sem, out_sem = scratch
    loads = []
    for i, (half, part, k) in enumerate(items):
        q = 2 * half + part
        row = []
        for h in range(4):
            if half == 0:
                rows = one.at[h, q, :, (pos[1] + k) % 4]
            else:
                rows = one.at[h, q, (pos[0] + k) % 4]
            row.append((rows, buf_one.at[h, i]))
        row.append((arrays[i].at[indices[i]], buf_two.at[i]))
        if extras:
            row.append((extras[i].at[0], buf_extra.at[i]))
        loads.append(
            [pltpu.make_async_copy(src, dst, in_sem.at[i, j]) for j, (src, dst) in enumerate(row)]
        )
    for row in loads:
        for copy in row:
            copy.start()
    writes = []
    for i in range(count):
        for copy in loads[i]:
            copy.wait()
        other = chunk(buf_one, i)
        own = buf_two[i].reshape(other.shape)
        value = back(own, other, weight[...], 3, 0, vec)
        if extras:
            value = total(value, buf_extra[i].reshape(other.shape))
        parts[i] = value.reshape(parts.shape[1:])
        writes.append(pltpu.make_async_copy(parts.at[i], outs[i].at[0], out_sem.at[i]))
        writes[-1].start()
    for copy in writes:
        copy.wait()


def back_two(pos, one, pieces, weight, vec, items, extras=()):
    rows, lanes = one.shape[4:]
    width = 4 * lanes
    count = len(items)
    mine = [pieces[4 * half + -k % 4][part] for half, part, k in items]
    anywhere = pl.BlockSpec(memory_space=pl.ANY)
    return pl.pallas_call(
        functools.partial(back_two_kernel, items, [piece[1] for piece in mine]),
        in_specs=[spec(SMEM)] + [anywhere] * (1 + count) + [spec()] * 2 + [anywhere] * len(extras),
        out_specs=[anywhere] * count,
        out_shape=[jax.ShapeDtypeStruct((1, 4, rows, width), jnp.bfloat16)] * count,
        scratch_shapes=[
            VMEM((4, count, 4, rows, lanes), jnp.bfloat16),
            VMEM((count, 4, rows, width), jnp.bfloat16),
            VMEM((count, 4, rows, width), jnp.bfloat16),
            VMEM((count, 4, rows, width), jnp.bfloat16),
            pltpu.SemaphoreType.DMA((count, 6)),
            pltpu.SemaphoreType.DMA((count,)),
        ],
        cost_estimate=pl.CostEstimate(
            flops=8 * count * rows * width * width,
            bytes_accessed=24 * count * rows * width,
            transcendentals=0,
        ),
        compiler_params=pltpu.CompilerParams(vmem_limit_bytes=LIMIT),
        name="back_two",
    )(pos, one, *[piece[0] for piece in mine], weight, vec, *extras)


def gather_ring(value, axis):
    behind = lax.ppermute(value, axis, shift(1))
    ahead = lax.ppermute(value, axis, shift(3))
    far = [
        lax.ppermute(behind[0:1], axis, shift(1)),
        lax.ppermute(ahead[1:2], axis, shift(3)),
    ]
    return [[(value, 0), (value, 1)], [(behind, 0), (behind, 1)], [(far[0], 0), (far[1], 0)]] + [
        [(ahead, 0), (ahead, 1)]
    ]


def put(buffer, piece, index):
    return lax.dynamic_update_index_in_dim(buffer, piece, index, 1)


def local(view_one, view_two):
    x, y = lax.axis_index("x"), lax.axis_index("y")
    zl, c, zh = lax.axis_index("zl"), lax.axis_index("c"), lax.axis_index("zh")
    slot = zl * 2 + c
    q = slot.astype(jnp.int32).reshape(1)
    pos = jnp.stack([x, y, zh * 4 + slot]).astype(jnp.int32)
    rows = view_one.shape[0]
    width = view_one.shape[1] // 4
    lanes = width // 4
    with jax.named_scope("relayout"):
        blocks, *pieces = split(q, view_one, view_two)
        for k in (1, 2, 3):
            pieces[k] = lax.ppermute(pieces[k], AXES, near(k))
        own_one = lax.all_to_all(blocks, ("x", "y"), 0, 0, tiled=True)
        a, b = join(q, pieces)
        own_one, a, b = lax.optimization_barrier((own_one, a, b))
    with jax.named_scope("gather_one"):
        first = lax.all_gather(own_one.reshape(16 * rows, lanes), COLS, tiled=True)
    with jax.named_scope("gather_two"):
        low = jnp.zeros((2, 4, rows, width), view_two.dtype)
        high = jnp.zeros((2, 4, rows, width), view_two.dtype)
        for k in (0, 1, 3, 2):
            low = put(low, lax.ppermute(a, "x", shift(k)) if k else a, (x - k) % 4)
            high = put(high, lax.ppermute(b, "y", shift(k)) if k else b, (y - k) % 4)
        low, high = lax.optimization_barrier((low, high))
        gathered = gather_ring(low, "y") + gather_ring(high, "x")
    first = first.reshape(4, 4, 4, 4, rows, lanes)
    part_one, slope, vec = tile_work(pos, first, gathered)
    with jax.named_scope("scatter_one"):
        grad_one = lax.psum_scatter(part_one.reshape(256 * rows, lanes), COLS, tiled=True)
    with jax.named_scope("scatter_two"):
        axes = ("y", "x")
        work = functools.partial(back_two, pos, first, gathered, slope, vec)

        def send(values, items):
            return [
                lax.ppermute(value, axes[half], shift(k))
                for value, (half, _, k) in zip(values, items)
            ]

        far = work([(0, 0, 2), (0, 1, 2), (1, 0, 2), (1, 1, 2)])
        plain_items = [(0, 0, 3), (0, 1, 1), (1, 0, 3), (1, 1, 1)]
        added_items = [(0, 0, 1), (0, 1, 3), (1, 0, 1), (1, 1, 3)]
        far = send(far, added_items)
        plain = send(work(plain_items), plain_items)
        added = send(work(added_items, far), added_items)
        own = work([(0, 0, 0), (0, 1, 0), (1, 0, 0), (1, 1, 0)])
        low = list(sum_pick(pos[0:1], [own[0], plain[0], added[0], own[1], plain[1], added[1]]))
        high = list(sum_pick(pos[1:2], [own[2], plain[2], added[2], own[3], plain[3], added[3]]))
        for k in (1, 3, 2):
            low[k] = lax.ppermute(low[k], "x", shift(k))
            high[k] = lax.ppermute(high[k], "y", shift(k))
    with jax.named_scope("relayout_back"):
        grad_one, *pieces = lax.optimization_barrier((grad_one, *unjoin(q, low, high)))
        for k in (1, 2, 3):
            pieces[k] = lax.ppermute(pieces[k], AXES, near(k))
        grad_one = lax.all_to_all(grad_one.reshape(16, rows, lanes), ("x", "y"), 0, 0, tiled=True)
        return tuple(unsplit(q, grad_one, pieces))


def solution(mesh):
    grid = Mesh(mesh.devices.reshape(SIZES), AXES)
    spread = P(("x", "zl", "y", "c"), "zh")
    return jax.shard_map(
        local, mesh=grid, in_specs=(spread, spread), out_specs=(spread, spread), check_vma=False
    )
```

```python
import functools
import itertools

import jax
import jax.numpy as jnp
from jax import lax
from jax.experimental import pallas as pl
from jax.experimental.pallas import tpu as pltpu
from jax.sharding import Mesh
from jax.sharding import PartitionSpec as P

EPSILON = 1e-05
OFF_WEIGHT = 0.0051
SIZES = (4, 2, 4, 2, 4)
AXES = ("x", "zl", "y", "c", "zh")
COLS = ("zh", "zl", "c")
VMEM = pltpu.VMEM
LIMIT = 58 * 2**20
SMALL = 12 * 2**20
SMEM = pltpu.SMEM


def device(x, zl, y, c, zh):
    return (((x * 2 + zl) * 4 + y) * 2 + c) * 4 + zh


def near(k):
    out = []
    for x, zl, y, c, zh in itertools.product(*map(range, SIZES)):
        q = (zl * 2 + c) ^ k
        out.append((device(x, zl, y, c, zh), device(x, q // 2, y, q % 2, zh)))
    return out


def shift(k):
    return [(i, (i + k) % 4) for i in range(4)]


def spec(space=VMEM):
    return pl.BlockSpec(memory_space=space)


def split_kernel(q_ref, one, two, blocks, *outs):
    q = q_ref[0]
    width = two.shape[1] // 4
    for k, out in enumerate(outs):
        cols = pl.ds(pl.multiple_of((q ^ k) * width, width), width)
        out[...] = two[:, cols]
    lanes = blocks.shape[2]
    for b in range(16):
        blocks[b] = one[:, b * lanes : (b + 1) * lanes]


def split(q, one, two):
    rows, width = one.shape
    shape = jax.ShapeDtypeStruct((rows, width // 4), one.dtype)
    return pl.pallas_call(
        split_kernel,
        out_shape=[jax.ShapeDtypeStruct((16, rows, width // 16), one.dtype)] + [shape] * 4,
        in_specs=[spec(SMEM), spec(), spec()],
        out_specs=[spec()] * 5,
        compiler_params=pltpu.CompilerParams(vmem_limit_bytes=SMALL),
        name="split",
    )(q, one, two)


def join_kernel(q_ref, p0, p1, p2, p3, low, high):
    q = q_ref[0]
    for k, piece in enumerate((p0, p1, p2, p3)):
        at = q ^ k

        @pl.when(at < 2)
        def _():
            low[at & 1] = piece[...]

        @pl.when(at >= 2)
        def _():
            high[at & 1] = piece[...]


def join(q, pieces):
    shape = jax.ShapeDtypeStruct((2,) + pieces[0].shape, pieces[0].dtype)
    return pl.pallas_call(
        join_kernel,
        out_shape=[shape] * 2,
        in_specs=[spec(SMEM)] + [spec()] * 4,
        out_specs=[spec()] * 2,
        compiler_params=pltpu.CompilerParams(vmem_limit_bytes=SMALL),
        name="join",
    )(q, *pieces)


def total(*refs):
    return functools.reduce(jnp.add, [ref.astype(jnp.float32) for ref in refs]).astype(jnp.bfloat16)


def sum_pick_kernel(me, *refs):
    for k, out in enumerate(refs[6:]):
        at = (me[0] + k) % 4
        out[0] = total(*[ref[0, at] for ref in refs[:3]])
        out[1] = total(*[ref[0, at] for ref in refs[3:6]])


def sum_pick(me, terms):
    _, _, rows, width = terms[0].shape
    return pl.pallas_call(
        sum_pick_kernel,
        out_shape=[jax.ShapeDtypeStruct((2, rows, width), jnp.bfloat16)] * 4,
        in_specs=[spec(SMEM)] + [spec()] * 6,
        out_specs=[spec()] * 4,
        compiler_params=pltpu.CompilerParams(vmem_limit_bytes=SMALL),
        name="sum_pick",
    )(me, *terms)


def unjoin_kernel(q_ref, *refs):
    q = q_ref[0]
    low, high, outs = refs[:4], refs[4:8], refs[8:]
    for k, out in enumerate(outs):
        at = q ^ k

        @pl.when(at < 2)
        def _():
            out[...] = total(*[ref[at & 1] for ref in low])

        @pl.when(at >= 2)
        def _():
            out[...] = total(*[ref[at & 1] for ref in high])


def unjoin(q, low, high):
    return pl.pallas_call(
        unjoin_kernel,
        out_shape=[jax.ShapeDtypeStruct(low[0].shape[1:], jnp.bfloat16)] * 4,
        in_specs=[spec(SMEM)] + [spec()] * 8,
        out_specs=[spec()] * 4,
        compiler_params=pltpu.CompilerParams(vmem_limit_bytes=SMALL),
        name="unjoin",
    )(q, *low, *high)


def unsplit_kernel(q_ref, blocks, p0, p1, p2, p3, one, two):
    q = q_ref[0]
    width = p0.shape[1]
    for k, piece in enumerate((p0, p1, p2, p3)):
        cols = pl.ds(pl.multiple_of((q ^ k) * width, width), width)
        two[:, cols] = piece[...]
    lanes = blocks.shape[2]
    for b in range(16):
        one[:, b * lanes : (b + 1) * lanes] = blocks[b]


def unsplit(q, blocks, pieces):
    rows, width = pieces[0].shape
    shape = jax.ShapeDtypeStruct((rows, 4 * width), pieces[0].dtype)
    return pl.pallas_call(
        unsplit_kernel,
        out_shape=[shape] * 2,
        in_specs=[spec(SMEM)] + [spec()] * 5,
        out_specs=[spec()] * 2,
        compiler_params=pltpu.CompilerParams(vmem_limit_bytes=SMALL),
        name="unsplit",
    )(q, blocks, *pieces)


def column(row):
    return jnp.broadcast_to(row, (8, row.shape[1])).T[:, 0:1]


def line(col):
    return jnp.broadcast_to(col, (col.shape[0], 128)).T[0:1, :]


def chunk(buffer, *at):
    blocks = [buffer[(h,) + at] for h in range(4)]
    return jnp.concatenate([block.reshape(-1, block.shape[-1]) for block in blocks], 1)


def back(own, other, weight, own_at, other_at, vec):
    mean_own, inv_own, proj_own = (vec[own_at + i : own_at + i + 1, :] for i in range(3))
    mean_other, inv_other = (vec[other_at + i : other_at + i + 1, :] for i in range(2))
    rounded = ((other.astype(jnp.float32) - mean_other) * inv_other).astype(jnp.bfloat16)
    product = jnp.dot(rounded, weight, preferred_element_type=jnp.float32)
    slant = inv_own * inv_own * proj_own
    return (inv_own * product - (own.astype(jnp.float32) - mean_own) * slant).astype(jnp.bfloat16)


def finish(count, pos, acc, sums, lanes):
    mean_one = jnp.sum(sums[0], 0, keepdims=True) / count
    mean_two = jnp.sum(sums[2], 0, keepdims=True) / count
    square_one = jnp.sum(sums[1], 0, keepdims=True) / count
    square_two = jnp.sum(sums[3], 0, keepdims=True) / count
    inv_one = lax.rsqrt(square_one - mean_one * mean_one + EPSILON)
    inv_two = lax.rsqrt(square_two - mean_two * mean_two + EPSILON)
    corr = (acc[...] / count - column(mean_one) * mean_two) * (column(inv_one) * inv_two)
    row = lax.broadcasted_iota(jnp.int32, corr.shape, 0)
    row = (row // lanes) * (16 * lanes) + (pos[0] * 4 + pos[1]) * lanes + row % lanes
    col = lax.broadcasted_iota(jnp.int32, corr.shape, 1) + pos[2] * corr.shape[1]
    slope = jnp.where(row == col, -2.0 * (1.0 - corr), 2.0 * OFF_WEIGHT * corr)
    weight = slope * corr
    proj_one = line(jnp.sum(weight, 1, keepdims=True))
    proj_two = jnp.sum(weight, 0, keepdims=True)
    rows = [mean_one, inv_one, proj_one, mean_two, inv_two, proj_two, proj_one, proj_two]
    return slope, jnp.concatenate(rows, 0)


def tile_kernel(count, places, pos, one, *refs):
    arrays, refs = refs[: len(places)], refs[len(places) :]
    part_out, slope_out, vec_out, buf_one, buf_two, acc, sums, turned, parts, in_sem, out_sem = refs
    lanes = one.shape[-1]
    loads = [[], [], [], []]
    for q in range(4):
        for h in range(4):
            loads[q].append((one.at[h, q], buf_one.at[h, q]))
    for ref, place in zip(arrays, places):
        q, k, index = place
        if q < 2:
            target = buf_two.at[q, :, (pos[1] - k) % 4]
        else:
            target = buf_two.at[q, (pos[0] - k) % 4]
        loads[q].append((ref.at[index], target))
    loads = [
        [pltpu.make_async_copy(src, dst, in_sem.at[q, i]) for i, (src, dst) in enumerate(row)]
        for q, row in enumerate(loads)
    ]
    for row in loads:
        for copy in row:
            copy.start()
    acc[...] = jnp.zeros_like(acc)
    sums[...] = jnp.zeros_like(sums)
    for q in range(4):
        for copy in loads[q]:
            copy.wait()

        @pl.loop(0, 4, unroll=4)
        def _(y):
            left = chunk(buf_one, q, slice(None), y)
            right = buf_two[q, :, y].reshape(left.shape)
            acc[...] += lax.dot_general(
                left, right, (((0,), (0,)), ((), ())), preferred_element_type=jnp.float32
            )
            for at, block in ((0, left), (2, right)):
                value = block.astype(jnp.float32).reshape(block.shape[0] // 8, 8, block.shape[1])
                sums[at] += jnp.sum(value, 0)
                sums[at + 1] += jnp.sum(value * value, 0)

    slope, vec = finish(count, pos, acc, sums, lanes)
    slope_out[...] = slope.astype(jnp.bfloat16)
    turned[...] = slope.T.astype(jnp.bfloat16)
    vec_out[...] = vec

    def write(step, h):
        rows = part_out.at[h, step // 4, :, step % 4]
        return pltpu.make_async_copy(parts.at[step % 4, h], rows, out_sem.at[step % 4, h])

    @pl.loop(0, 16)
    def _(step):
        @pl.when(step >= 4)
        def _():
            for h in range(4):
                write(step - 4, h).wait()

        q, y = step // 4, step % 4
        own = chunk(buf_one, q, slice(None), y)
        other = buf_two[q, :, y].reshape(own.shape)
        part = back(own, other, turned[...], 0, 3, vec_out)
        for h in range(4):
            block = part[:, h * lanes : (h + 1) * lanes]
            parts[step % 4, h] = block.reshape(parts.shape[2:])
            write(step, h).start()

    for step in range(12, 16):
        for h in range(4):
            write(step, h).wait()


def tile_work(pos, one, pieces):
    rows, lanes = one.shape[4:]
    width = 4 * lanes
    count = 64 * rows
    arrays, places = [], []
    for at in range(8):
        for part in range(2):
            array, index = pieces[at][part]
            arrays.append(array)
            places.append((2 * (at // 4) + part, at % 4, index))
    anywhere = pl.BlockSpec(memory_space=pl.ANY)
    return pl.pallas_call(
        functools.partial(tile_kernel, count, places),
        in_specs=[spec(SMEM)] + [anywhere] * 17,
        out_specs=[anywhere, spec(), spec()],
        out_shape=[
            jax.ShapeDtypeStruct(one.shape, jnp.bfloat16),
            jax.ShapeDtypeStruct((width, width), jnp.bfloat16),
            jax.ShapeDtypeStruct((8, width), jnp.float32),
        ],
        scratch_shapes=[
            VMEM((4, 4, 4, 4, rows, lanes), jnp.bfloat16),
            VMEM((4, 4, 4, rows, width), jnp.bfloat16),
            VMEM((width, width), jnp.float32),
            VMEM((4, 8, width), jnp.float32),
            VMEM((width, width), jnp.bfloat16),
            VMEM((4, 4, 4, rows, lanes), jnp.bfloat16),
            pltpu.SemaphoreType.DMA((4, 8)),
            pltpu.SemaphoreType.DMA((4, 4)),
        ],
        cost_estimate=pl.CostEstimate(
            flops=4 * count * width * width, bytes_accessed=6 * count * width, transcendentals=0
        ),
        compiler_params=pltpu.CompilerParams(vmem_limit_bytes=LIMIT),
        name="tile",
    )(pos, one, *arrays)


def back_two_kernel(items, indices, pos, one, *refs):
    count = len(items)
    arrays, (weight, vec), refs = refs[:count], refs[count : count + 2], refs[count + 2 :]
    extras, outs, scratch = refs[: -count - 6], refs[-count - 6 : -6], refs[-6:]
    buf_one, buf_two, buf_extra, parts, in_sem, out_sem = scratch
    loads = []
    for i, (half, part, k) in enumerate(items):
        q = 2 * half + part
        row = []
        for h in range(4):
            if half == 0:
                rows = one.at[h, q, :, (pos[1] + k) % 4]
            else:
                rows = one.at[h, q, (pos[0] + k) % 4]
            row.append((rows, buf_one.at[h, i]))
        row.append((arrays[i].at[indices[i]], buf_two.at[i]))
        if extras:
            row.append((extras[i].at[0], buf_extra.at[i]))
        loads.append(
            [pltpu.make_async_copy(src, dst, in_sem.at[i, j]) for j, (src, dst) in enumerate(row)]
        )
    for row in loads:
        for copy in row:
            copy.start()
    writes = []
    for i in range(count):
        for copy in loads[i]:
            copy.wait()
        other = chunk(buf_one, i)
        own = buf_two[i].reshape(other.shape)
        value = back(own, other, weight[...], 3, 0, vec)
        if extras:
            value = total(value, buf_extra[i].reshape(other.shape))
        parts[i] = value.reshape(parts.shape[1:])
        writes.append(pltpu.make_async_copy(parts.at[i], outs[i].at[0], out_sem.at[i]))
        writes[-1].start()
    for copy in writes:
        copy.wait()


def back_two(pos, one, pieces, weight, vec, items, extras=()):
    rows, lanes = one.shape[4:]
    width = 4 * lanes
    count = len(items)
    mine = [pieces[4 * half + -k % 4][part] for half, part, k in items]
    anywhere = pl.BlockSpec(memory_space=pl.ANY)
    return pl.pallas_call(
        functools.partial(back_two_kernel, items, [piece[1] for piece in mine]),
        in_specs=[spec(SMEM)] + [anywhere] * (1 + count) + [spec()] * 2 + [anywhere] * len(extras),
        out_specs=[anywhere] * count,
        out_shape=[jax.ShapeDtypeStruct((1, 4, rows, width), jnp.bfloat16)] * count,
        scratch_shapes=[
            VMEM((4, count, 4, rows, lanes), jnp.bfloat16),
            VMEM((count, 4, rows, width), jnp.bfloat16),
            VMEM((count, 4, rows, width), jnp.bfloat16),
            VMEM((count, 4, rows, width), jnp.bfloat16),
            pltpu.SemaphoreType.DMA((count, 6)),
            pltpu.SemaphoreType.DMA((count,)),
        ],
        cost_estimate=pl.CostEstimate(
            flops=8 * count * rows * width * width,
            bytes_accessed=24 * count * rows * width,
            transcendentals=0,
        ),
        compiler_params=pltpu.CompilerParams(vmem_limit_bytes=LIMIT),
        name="back_two",
    )(pos, one, *[piece[0] for piece in mine], weight, vec, *extras)


def gather_ring(value, axis):
    behind = lax.ppermute(value, axis, shift(1))
    ahead = lax.ppermute(value, axis, shift(3))
    far = [
        lax.ppermute(behind[0:1], axis, shift(1)),
        lax.ppermute(ahead[1:2], axis, shift(3)),
    ]
    return [[(value, 0), (value, 1)], [(behind, 0), (behind, 1)], [(far[0], 0), (far[1], 0)]] + [
        [(ahead, 0), (ahead, 1)]
    ]


def put(buffer, piece, index):
    return lax.dynamic_update_index_in_dim(buffer, piece, index, 1)


def local(view_one, view_two):
    x, y = lax.axis_index("x"), lax.axis_index("y")
    zl, c, zh = lax.axis_index("zl"), lax.axis_index("c"), lax.axis_index("zh")
    slot = zl * 2 + c
    q = slot.astype(jnp.int32).reshape(1)
    pos = jnp.stack([x, y, zh * 4 + slot]).astype(jnp.int32)
    rows = view_one.shape[0]
    width = view_one.shape[1] // 4
    lanes = width // 4
    with jax.named_scope("relayout"):
        blocks, *pieces = split(q, view_one, view_two)
        for k in (1, 2, 3):
            pieces[k] = lax.ppermute(pieces[k], AXES, near(k))
        own_one = lax.all_to_all(blocks, ("x", "y"), 0, 0, tiled=True)
        a, b = join(q, pieces)
        own_one, a, b = lax.optimization_barrier((own_one, a, b))
    with jax.named_scope("gather_one"):
        first = lax.all_gather(own_one.reshape(16 * rows, lanes), COLS, tiled=True)
    with jax.named_scope("gather_two"):
        low = jnp.zeros((2, 4, rows, width), view_two.dtype)
        high = jnp.zeros((2, 4, rows, width), view_two.dtype)
        for k in (0, 1, 3, 2):
            low = put(low, lax.ppermute(a, "x", shift(k)) if k else a, (x - k) % 4)
            high = put(high, lax.ppermute(b, "y", shift(k)) if k else b, (y - k) % 4)
        low, high = lax.optimization_barrier((low, high))
        gathered = gather_ring(low, "y") + gather_ring(high, "x")
    first = first.reshape(4, 4, 4, 4, rows, lanes)
    part_one, slope, vec = tile_work(pos, first, gathered)
    with jax.named_scope("scatter_one"):
        grad_one = lax.psum_scatter(part_one.reshape(256 * rows, lanes), COLS, tiled=True)
    with jax.named_scope("scatter_two"):
        axes = ("y", "x")
        work = functools.partial(back_two, pos, first, gathered, slope, vec)

        def send(values, items):
            return [
                lax.ppermute(value, axes[half], shift(k))
                for value, (half, _, k) in zip(values, items)
            ]

        far = work([(0, 0, 2), (0, 1, 2), (1, 0, 2), (1, 1, 2)])
        plain_items = [(0, 0, 3), (0, 1, 1), (1, 0, 3), (1, 1, 1)]
        added_items = [(0, 0, 1), (0, 1, 3), (1, 0, 1), (1, 1, 3)]
        far = send(far, added_items)
        plain = send(work(plain_items), plain_items)
        added = send(work(added_items, far), added_items)
        own = work([(0, 0, 0), (0, 1, 0), (1, 0, 0), (1, 1, 0)])
        low = list(sum_pick(pos[0:1], [own[0], plain[0], added[0], own[1], plain[1], added[1]]))
        high = list(sum_pick(pos[1:2], [own[2], plain[2], added[2], own[3], plain[3], added[3]]))
        for k in (1, 3, 2):
            low[k] = lax.ppermute(low[k], "x", shift(k))
            high[k] = lax.ppermute(high[k], "y", shift(k))
    with jax.named_scope("relayout_back"):
        pieces = list(unjoin(q, low, high))
        for k in (1, 2, 3):
            pieces[k] = lax.ppermute(pieces[k], AXES, near(k))
        grad_one, pieces[1] = lax.optimization_barrier((grad_one, pieces[1]))
        grad_one = lax.all_to_all(grad_one.reshape(16, rows, lanes), ("x", "y"), 0, 0, tiled=True)
        return tuple(unsplit(q, grad_one, pieces))


def solution(mesh):
    grid = Mesh(mesh.devices.reshape(SIZES), AXES)
    spread = P(("x", "zl", "y", "c"), "zh")
    return jax.shard_map(
        local, mesh=grid, in_specs=(spread, spread), out_specs=(spread, spread), check_vma=False
    )
```

```python
import functools
import itertools

import jax
import jax.numpy as jnp
from jax import lax
from jax.experimental import pallas as pl
from jax.experimental.pallas import tpu as pltpu
from jax.sharding import Mesh
from jax.sharding import PartitionSpec as P

EPSILON = 1e-05
OFF_WEIGHT = 0.0051
SIZES = (4, 2, 4, 2, 4)
AXES = ("x", "zl", "y", "c", "zh")
COLS = ("zh", "zl", "c")
VMEM = pltpu.VMEM
LIMIT = 58 * 2**20
SMALL = 12 * 2**20
SMEM = pltpu.SMEM


def device(x, zl, y, c, zh):
    return (((x * 2 + zl) * 4 + y) * 2 + c) * 4 + zh


def near(k):
    out = []
    for x, zl, y, c, zh in itertools.product(*map(range, SIZES)):
        q = (zl * 2 + c) ^ k
        out.append((device(x, zl, y, c, zh), device(x, q // 2, y, q % 2, zh)))
    return out


def shift(k):
    return [(i, (i + k) % 4) for i in range(4)]


def spec(space=VMEM):
    return pl.BlockSpec(memory_space=space)


def split_kernel(q_ref, one, two, blocks, *outs):
    q = q_ref[0]
    width = two.shape[1] // 4
    for k, out in enumerate(outs):
        cols = pl.ds(pl.multiple_of((q ^ k) * width, width), width)
        out[...] = two[:, cols]
    lanes = blocks.shape[2]
    for b in range(16):
        blocks[b] = one[:, b * lanes : (b + 1) * lanes]


def split(q, one, two):
    rows, width = one.shape
    shape = jax.ShapeDtypeStruct((rows, width // 4), one.dtype)
    return pl.pallas_call(
        split_kernel,
        out_shape=[jax.ShapeDtypeStruct((16, rows, width // 16), one.dtype)] + [shape] * 4,
        in_specs=[spec(SMEM), spec(), spec()],
        out_specs=[spec()] * 5,
        compiler_params=pltpu.CompilerParams(vmem_limit_bytes=SMALL),
        name="split",
    )(q, one, two)


def join_kernel(q_ref, p0, p1, p2, p3, low, high):
    q = q_ref[0]
    for k, piece in enumerate((p0, p1, p2, p3)):
        at = q ^ k

        @pl.when(at < 2)
        def _():
            low[at & 1] = piece[...]

        @pl.when(at >= 2)
        def _():
            high[at & 1] = piece[...]


def join(q, pieces):
    shape = jax.ShapeDtypeStruct((2,) + pieces[0].shape, pieces[0].dtype)
    return pl.pallas_call(
        join_kernel,
        out_shape=[shape] * 2,
        in_specs=[spec(SMEM)] + [spec()] * 4,
        out_specs=[spec()] * 2,
        compiler_params=pltpu.CompilerParams(vmem_limit_bytes=SMALL),
        name="join",
    )(q, *pieces)


def total(*refs):
    return functools.reduce(jnp.add, [ref.astype(jnp.float32) for ref in refs]).astype(jnp.bfloat16)


def sum_pick_kernel(me, *refs):
    for k, out in enumerate(refs[6:]):
        at = (me[0] + k) % 4
        out[0] = total(*[ref[0, at] for ref in refs[:3]])
        out[1] = total(*[ref[0, at] for ref in refs[3:6]])


def sum_pick(me, terms):
    _, _, rows, width = terms[0].shape
    return pl.pallas_call(
        sum_pick_kernel,
        out_shape=[jax.ShapeDtypeStruct((2, rows, width), jnp.bfloat16)] * 4,
        in_specs=[spec(SMEM)] + [spec()] * 6,
        out_specs=[spec()] * 4,
        compiler_params=pltpu.CompilerParams(vmem_limit_bytes=SMALL),
        name="sum_pick",
    )(me, *terms)


def unjoin_kernel(q_ref, *refs):
    q = q_ref[0]
    low, high, outs = refs[:4], refs[4:8], refs[8:]
    for k, out in enumerate(outs):
        at = q ^ k

        @pl.when(at < 2)
        def _():
            out[...] = total(*[ref[at & 1] for ref in low])

        @pl.when(at >= 2)
        def _():
            out[...] = total(*[ref[at & 1] for ref in high])


def unjoin(q, low, high):
    return pl.pallas_call(
        unjoin_kernel,
        out_shape=[jax.ShapeDtypeStruct(low[0].shape[1:], jnp.bfloat16)] * 4,
        in_specs=[spec(SMEM)] + [spec()] * 8,
        out_specs=[spec()] * 4,
        compiler_params=pltpu.CompilerParams(vmem_limit_bytes=SMALL),
        name="unjoin",
    )(q, *low, *high)


def unsplit_kernel(q_ref, blocks, p0, p1, p2, p3, one, two):
    q = q_ref[0]
    width = p0.shape[1]
    for k, piece in enumerate((p0, p1, p2, p3)):
        cols = pl.ds(pl.multiple_of((q ^ k) * width, width), width)
        two[:, cols] = piece[...]
    lanes = blocks.shape[2]
    for b in range(16):
        one[:, b * lanes : (b + 1) * lanes] = blocks[b]


def unsplit(q, blocks, pieces):
    rows, width = pieces[0].shape
    shape = jax.ShapeDtypeStruct((rows, 4 * width), pieces[0].dtype)
    return pl.pallas_call(
        unsplit_kernel,
        out_shape=[shape] * 2,
        in_specs=[spec(SMEM)] + [spec()] * 5,
        out_specs=[spec()] * 2,
        compiler_params=pltpu.CompilerParams(vmem_limit_bytes=SMALL),
        name="unsplit",
    )(q, blocks, *pieces)


def line(col):
    return jnp.broadcast_to(col, (col.shape[0], 128)).T[0:1, :]


def chunk(buffer, *at):
    blocks = [buffer[(h,) + at] for h in range(4)]
    return jnp.concatenate([block.reshape(-1, block.shape[-1]) for block in blocks], 1)


def back(own, other, weight, own_at, other_at, vec):
    mean_own, inv_own, proj_own = (vec[own_at + i : own_at + i + 1, :] for i in range(3))
    mean_other, inv_other = (vec[other_at + i : other_at + i + 1, :] for i in range(2))
    rounded = ((other.astype(jnp.float32) - mean_other) * inv_other).astype(jnp.bfloat16)
    product = jnp.dot(rounded, weight, preferred_element_type=jnp.float32)
    slant = inv_own * inv_own * proj_own
    return (inv_own * product - (own.astype(jnp.float32) - mean_own) * slant).astype(jnp.bfloat16)


def moments(total, square, count):
    mean = jnp.sum(total, 0, keepdims=True) / count
    inverse = lax.rsqrt(jnp.sum(square, 0, keepdims=True) / count - mean * mean + EPSILON)
    return mean, inverse


def finish(count, pos, acc, sums, lanes, cols, slope_out, turned, vec_out):
    for at in range(2):
        mean, inverse = moments(sums[2 * at], sums[2 * at + 1], count)
        vec_out[3 * at : 3 * at + 1, :] = mean
        vec_out[3 * at + 1 : 3 * at + 2, :] = inverse
    vec_out[5:8, :] = jnp.zeros((3, acc.shape[1]), jnp.float32)
    cols[...] = vec_out[...].T

    @pl.loop(0, 4)
    def _(r):
        rows = pl.ds(pl.multiple_of(r * lanes, lanes), lanes)
        mean_one, inv_one = cols[rows, 0:1], cols[rows, 1:2]
        mean_two, inv_two = vec_out[3:4, :], vec_out[4:5, :]
        corr = (acc[rows, :] / count - mean_one * mean_two) * (inv_one * inv_two)
        row = lax.broadcasted_iota(jnp.int32, corr.shape, 0)
        row += r * (16 * lanes) + (pos[0] * 4 + pos[1]) * lanes
        col = lax.broadcasted_iota(jnp.int32, corr.shape, 1) + pos[2] * corr.shape[1]
        slope = jnp.where(row == col, -2.0 * (1.0 - corr), 2.0 * OFF_WEIGHT * corr)
        weight = slope * corr
        vec_out[2:3, rows] = line(jnp.sum(weight, 1, keepdims=True))
        vec_out[5:6, :] += jnp.sum(weight, 0, keepdims=True)
        slope_out[rows, :] = slope.astype(jnp.bfloat16)
        turned[:, rows] = slope.T.astype(jnp.bfloat16)


def tile_kernel(count, places, pos, one, *refs):
    arrays, refs = refs[: len(places)], refs[len(places) :]
    part_out, slope_out, vec_out, buf_one, buf_two, acc, sums = refs[:7]
    cols, turned, parts, in_sem, out_sem = refs[7:]
    lanes = one.shape[-1]
    loads = [[], [], [], []]
    for q in range(4):
        for h in range(4):
            loads[q].append((one.at[h, q], buf_one.at[h, q]))
    for ref, place in zip(arrays, places):
        q, k, index = place
        if q < 2:
            target = buf_two.at[q, :, (pos[1] - k) % 4]
        else:
            target = buf_two.at[q, (pos[0] - k) % 4]
        loads[q].append((ref.at[index], target))
    loads = [
        [pltpu.make_async_copy(src, dst, in_sem.at[q, i]) for i, (src, dst) in enumerate(row)]
        for q, row in enumerate(loads)
    ]
    for row in loads:
        for copy in row:
            copy.start()
    acc[...] = jnp.zeros_like(acc)
    sums[...] = jnp.zeros_like(sums)

    @pl.loop(0, 4)
    def _(q):
        for h in range(4):
            pltpu.make_async_copy(buf_one.at[h, q], buf_one.at[h, q], in_sem.at[q, h]).wait()
            pltpu.make_async_copy(buf_two.at[q, h], buf_two.at[q, h], in_sem.at[q, 4 + h]).wait()

        @pl.loop(0, 4, unroll=4)
        def _(y):
            left = chunk(buf_one, q, slice(None), y)
            right = buf_two[q, :, y].reshape(left.shape)
            acc[...] += lax.dot_general(
                left, right, (((0,), (0,)), ((), ())), preferred_element_type=jnp.float32
            )
            for at, block in ((0, left), (2, right)):
                value = block.astype(jnp.float32).reshape(block.shape[0] // 8, 8, block.shape[1])
                sums[at] += jnp.sum(value, 0)
                sums[at + 1] += jnp.sum(value * value, 0)

    finish(count, pos, acc, sums, lanes, cols, slope_out, turned, vec_out)

    def write(step, h):
        rows = part_out.at[h, step // 4, :, step % 4]
        return pltpu.make_async_copy(parts.at[step % 4, h], rows, out_sem.at[step % 4, h])

    @pl.loop(0, 16)
    def _(step):
        @pl.when(step >= 4)
        def _():
            for h in range(4):
                write(step - 4, h).wait()

        q, y = step // 4, step % 4
        own = chunk(buf_one, q, slice(None), y)
        other = buf_two[q, :, y].reshape(own.shape)
        part = back(own, other, turned[...], 0, 3, vec_out)
        for h in range(4):
            block = part[:, h * lanes : (h + 1) * lanes]
            parts[step % 4, h] = block.reshape(parts.shape[2:])
            write(step, h).start()

    for step in range(12, 16):
        for h in range(4):
            write(step, h).wait()


def tile_work(pos, one, pieces):
    rows, lanes = one.shape[4:]
    width = 4 * lanes
    count = 64 * rows
    arrays, places = [], []
    for at in range(8):
        for part in range(2):
            array, index = pieces[at][part]
            arrays.append(array)
            places.append((2 * (at // 4) + part, at % 4, index))
    anywhere = pl.BlockSpec(memory_space=pl.ANY)
    return pl.pallas_call(
        functools.partial(tile_kernel, count, places),
        in_specs=[spec(SMEM)] + [anywhere] * 17,
        out_specs=[anywhere, spec(), spec()],
        out_shape=[
            jax.ShapeDtypeStruct(one.shape, jnp.bfloat16),
            jax.ShapeDtypeStruct((width, width), jnp.bfloat16),
            jax.ShapeDtypeStruct((8, width), jnp.float32),
        ],
        scratch_shapes=[
            VMEM((4, 4, 4, 4, rows, lanes), jnp.bfloat16),
            VMEM((4, 4, 4, rows, width), jnp.bfloat16),
            VMEM((width, width), jnp.float32),
            VMEM((4, 8, width), jnp.float32),
            VMEM((width, 8), jnp.float32),
            VMEM((width, width), jnp.bfloat16),
            VMEM((4, 4, 4, rows, lanes), jnp.bfloat16),
            pltpu.SemaphoreType.DMA((4, 8)),
            pltpu.SemaphoreType.DMA((4, 4)),
        ],
        cost_estimate=pl.CostEstimate(
            flops=4 * count * width * width, bytes_accessed=6 * count * width, transcendentals=0
        ),
        compiler_params=pltpu.CompilerParams(vmem_limit_bytes=LIMIT),
        name="tile",
    )(pos, one, *arrays)


def back_two_kernel(items, indices, pos, one, *refs):
    count = len(items)
    arrays, (weight, vec), refs = refs[:count], refs[count : count + 2], refs[count + 2 :]
    extras, outs, scratch = refs[: -count - 6], refs[-count - 6 : -6], refs[-6:]
    buf_one, buf_two, buf_extra, parts, in_sem, out_sem = scratch
    loads = []
    for i, (half, part, k) in enumerate(items):
        q = 2 * half + part
        row = []
        for h in range(4):
            if half == 0:
                rows = one.at[h, q, :, (pos[1] + k) % 4]
            else:
                rows = one.at[h, q, (pos[0] + k) % 4]
            row.append((rows, buf_one.at[h, i]))
        row.append((arrays[i].at[indices[i]], buf_two.at[i]))
        if extras:
            row.append((extras[i].at[0], buf_extra.at[i]))
        loads.append(
            [pltpu.make_async_copy(src, dst, in_sem.at[i, j]) for j, (src, dst) in enumerate(row)]
        )
    for row in loads:
        for copy in row:
            copy.start()

    @pl.loop(0, count)
    def _(i):
        for h in range(4):
            pltpu.make_async_copy(buf_one.at[h, i], buf_one.at[h, i], in_sem.at[i, h]).wait()
        pltpu.make_async_copy(buf_two.at[i], buf_two.at[i], in_sem.at[i, 4]).wait()
        if extras:
            pltpu.make_async_copy(buf_extra.at[i], buf_extra.at[i], in_sem.at[i, 5]).wait()
        other = chunk(buf_one, i)
        own = buf_two[i].reshape(other.shape)
        value = back(own, other, weight[...], 3, 0, vec)
        if extras:
            value = total(value, buf_extra[i].reshape(other.shape))
        parts[i] = value.reshape(parts.shape[1:])
        for n in range(count):

            @pl.when(i == n)
            def _():
                pltpu.make_async_copy(parts.at[n], outs[n].at[0], out_sem.at[n]).start()

    for n in range(count):
        pltpu.make_async_copy(parts.at[n], outs[n].at[0], out_sem.at[n]).wait()


def back_two(pos, one, pieces, weight, vec, items, extras=()):
    rows, lanes = one.shape[4:]
    width = 4 * lanes
    count = len(items)
    mine = [pieces[4 * half + -k % 4][part] for half, part, k in items]
    anywhere = pl.BlockSpec(memory_space=pl.ANY)
    return pl.pallas_call(
        functools.partial(back_two_kernel, items, [piece[1] for piece in mine]),
        in_specs=[spec(SMEM)] + [anywhere] * (1 + count) + [spec()] * 2 + [anywhere] * len(extras),
        out_specs=[anywhere] * count,
        out_shape=[jax.ShapeDtypeStruct((1, 4, rows, width), jnp.bfloat16)] * count,
        scratch_shapes=[
            VMEM((4, count, 4, rows, lanes), jnp.bfloat16),
            VMEM((count, 4, rows, width), jnp.bfloat16),
            VMEM((count, 4, rows, width), jnp.bfloat16),
            VMEM((count, 4, rows, width), jnp.bfloat16),
            pltpu.SemaphoreType.DMA((count, 6)),
            pltpu.SemaphoreType.DMA((count,)),
        ],
        cost_estimate=pl.CostEstimate(
            flops=8 * count * rows * width * width,
            bytes_accessed=24 * count * rows * width,
            transcendentals=0,
        ),
        compiler_params=pltpu.CompilerParams(vmem_limit_bytes=LIMIT),
        name="back_two",
    )(pos, one, *[piece[0] for piece in mine], weight, vec, *extras)


def gather_ring(value, axis):
    behind = lax.ppermute(value, axis, shift(1))
    ahead = lax.ppermute(value, axis, shift(3))
    far = [
        lax.ppermute(behind[0:1], axis, shift(1)),
        lax.ppermute(ahead[1:2], axis, shift(3)),
    ]
    return [[(value, 0), (value, 1)], [(behind, 0), (behind, 1)], [(far[0], 0), (far[1], 0)]] + [
        [(ahead, 0), (ahead, 1)]
    ]


def put(buffer, piece, index):
    return lax.dynamic_update_index_in_dim(buffer, piece, index, 1)


def local(view_one, view_two):
    x, y = lax.axis_index("x"), lax.axis_index("y")
    zl, c, zh = lax.axis_index("zl"), lax.axis_index("c"), lax.axis_index("zh")
    slot = zl * 2 + c
    q = slot.astype(jnp.int32).reshape(1)
    pos = jnp.stack([x, y, zh * 4 + slot]).astype(jnp.int32)
    rows = view_one.shape[0]
    width = view_one.shape[1] // 4
    lanes = width // 4
    with jax.named_scope("relayout"):
        blocks, *pieces = split(q, view_one, view_two)
        for k in (1, 2, 3):
            pieces[k] = lax.ppermute(pieces[k], AXES, near(k))
        own_one = lax.all_to_all(blocks, ("x", "y"), 0, 0, tiled=True)
        a, b = join(q, pieces)
        own_one, a, b = lax.optimization_barrier((own_one, a, b))
    with jax.named_scope("gather_one"):
        first = lax.all_gather(own_one.reshape(16 * rows, lanes), COLS, tiled=True)
    with jax.named_scope("gather_two"):
        low = jnp.zeros((2, 4, rows, width), view_two.dtype)
        high = jnp.zeros((2, 4, rows, width), view_two.dtype)
        for k in (0, 1, 3, 2):
            low = put(low, lax.ppermute(a, "x", shift(k)) if k else a, (x - k) % 4)
            high = put(high, lax.ppermute(b, "y", shift(k)) if k else b, (y - k) % 4)
        low, high = lax.optimization_barrier((low, high))
        gathered = gather_ring(low, "y") + gather_ring(high, "x")
    first = first.reshape(4, 4, 4, 4, rows, lanes)
    part_one, slope, vec = tile_work(pos, first, gathered)
    with jax.named_scope("scatter_one"):
        grad_one = lax.psum_scatter(part_one.reshape(256 * rows, lanes), COLS, tiled=True)
    with jax.named_scope("scatter_two"):
        axes = ("y", "x")
        work = functools.partial(back_two, pos, first, gathered, slope, vec)

        def send(values, items):
            return [
                lax.ppermute(value, axes[half], shift(k))
                for value, (half, _, k) in zip(values, items)
            ]

        far = work([(0, 0, 2), (0, 1, 2), (1, 0, 2), (1, 1, 2)])
        plain_items = [(0, 0, 3), (0, 1, 1), (1, 0, 3), (1, 1, 1)]
        added_items = [(0, 0, 1), (0, 1, 3), (1, 0, 1), (1, 1, 3)]
        far = send(far, added_items)
        plain = send(work(plain_items), plain_items)
        added = send(work(added_items, far), added_items)
        own = work([(0, 0, 0), (0, 1, 0), (1, 0, 0), (1, 1, 0)])
        low = list(sum_pick(pos[0:1], [own[0], plain[0], added[0], own[1], plain[1], added[1]]))
        high = list(sum_pick(pos[1:2], [own[2], plain[2], added[2], own[3], plain[3], added[3]]))
        for k in (1, 3, 2):
            low[k] = lax.ppermute(low[k], "x", shift(k))
            high[k] = lax.ppermute(high[k], "y", shift(k))
    with jax.named_scope("relayout_back"):
        pieces = list(unjoin(q, low, high))
        for k in (1, 2, 3):
            pieces[k] = lax.ppermute(pieces[k], AXES, near(k))
        grad_one, pieces[1] = lax.optimization_barrier((grad_one, pieces[1]))
        grad_one = lax.all_to_all(grad_one.reshape(16, rows, lanes), ("x", "y"), 0, 0, tiled=True)
        return tuple(unsplit(q, grad_one, pieces))


def solution(mesh):
    grid = Mesh(mesh.devices.reshape(SIZES), AXES)
    spread = P(("x", "zl", "y", "c"), "zh")
    return jax.shard_map(
        local, mesh=grid, in_specs=(spread, spread), out_specs=(spread, spread), check_vma=False
    )
```

```python
import functools
import itertools

import jax
import jax.numpy as jnp
from jax import lax
from jax.experimental import pallas as pl
from jax.experimental.pallas import tpu as pltpu
from jax.sharding import Mesh
from jax.sharding import PartitionSpec as P

EPSILON = 1e-05
OFF_WEIGHT = 0.0051
SIZES = (4, 2, 4, 2, 4)
AXES = ("x", "zl", "y", "c", "zh")
COLS = ("zh", "zl", "c")
VMEM = pltpu.VMEM
LIMIT = 58 * 2**20
SMALL = 12 * 2**20
SMEM = pltpu.SMEM


def device(x, zl, y, c, zh):
    return (((x * 2 + zl) * 4 + y) * 2 + c) * 4 + zh


def near(k):
    out = []
    for x, zl, y, c, zh in itertools.product(*map(range, SIZES)):
        q = (zl * 2 + c) ^ k
        out.append((device(x, zl, y, c, zh), device(x, q // 2, y, q % 2, zh)))
    return out


def shift(k):
    return [(i, (i + k) % 4) for i in range(4)]


def spec(space=VMEM):
    return pl.BlockSpec(memory_space=space)


def split_kernel(q_ref, one, two, blocks, *outs):
    q = q_ref[0]
    width = two.shape[1] // 4
    for k, out in enumerate(outs):
        cols = pl.ds(pl.multiple_of((q ^ k) * width, width), width)
        out[...] = two[:, cols]
    lanes = blocks.shape[2]
    for b in range(16):
        blocks[b] = one[:, b * lanes : (b + 1) * lanes]


def split(q, one, two):
    rows, width = one.shape
    shape = jax.ShapeDtypeStruct((rows, width // 4), one.dtype)
    return pl.pallas_call(
        split_kernel,
        out_shape=[jax.ShapeDtypeStruct((16, rows, width // 16), one.dtype)] + [shape] * 4,
        in_specs=[spec(SMEM), spec(), spec()],
        out_specs=[spec()] * 5,
        compiler_params=pltpu.CompilerParams(vmem_limit_bytes=SMALL),
        name="split",
    )(q, one, two)


def join_kernel(q_ref, p0, p1, p2, p3, low, high):
    q = q_ref[0]
    for k, piece in enumerate((p0, p1, p2, p3)):
        at = q ^ k

        @pl.when(at < 2)
        def _():
            low[at & 1] = piece[...]

        @pl.when(at >= 2)
        def _():
            high[at & 1] = piece[...]


def join(q, pieces):
    shape = jax.ShapeDtypeStruct((2,) + pieces[0].shape, pieces[0].dtype)
    return pl.pallas_call(
        join_kernel,
        out_shape=[shape] * 2,
        in_specs=[spec(SMEM)] + [spec()] * 4,
        out_specs=[spec()] * 2,
        compiler_params=pltpu.CompilerParams(vmem_limit_bytes=SMALL),
        name="join",
    )(q, *pieces)


def total(*refs):
    return functools.reduce(jnp.add, [ref.astype(jnp.float32) for ref in refs]).astype(jnp.bfloat16)


def sum_pick_kernel(me, *refs):
    for k, out in enumerate(refs[6:]):
        at = (me[0] + k) % 4
        out[0] = total(*[ref[0, at] for ref in refs[:3]])
        out[1] = total(*[ref[0, at] for ref in refs[3:6]])


def sum_pick(me, terms):
    _, _, rows, width = terms[0].shape
    return pl.pallas_call(
        sum_pick_kernel,
        out_shape=[jax.ShapeDtypeStruct((2, rows, width), jnp.bfloat16)] * 4,
        in_specs=[spec(SMEM)] + [spec()] * 6,
        out_specs=[spec()] * 4,
        compiler_params=pltpu.CompilerParams(vmem_limit_bytes=SMALL),
        name="sum_pick",
    )(me, *terms)


def unjoin_kernel(q_ref, *refs):
    q = q_ref[0]
    low, high, outs = refs[:4], refs[4:8], refs[8:]
    for k, out in enumerate(outs):
        at = q ^ k

        @pl.when(at < 2)
        def _():
            out[...] = total(*[ref[at & 1] for ref in low])

        @pl.when(at >= 2)
        def _():
            out[...] = total(*[ref[at & 1] for ref in high])


def unjoin(q, low, high):
    return pl.pallas_call(
        unjoin_kernel,
        out_shape=[jax.ShapeDtypeStruct(low[0].shape[1:], jnp.bfloat16)] * 4,
        in_specs=[spec(SMEM)] + [spec()] * 8,
        out_specs=[spec()] * 4,
        compiler_params=pltpu.CompilerParams(vmem_limit_bytes=SMALL),
        name="unjoin",
    )(q, *low, *high)


def unsplit_kernel(q_ref, blocks, p0, p1, p2, p3, one, two):
    q = q_ref[0]
    width = p0.shape[1]
    for k, piece in enumerate((p0, p1, p2, p3)):
        cols = pl.ds(pl.multiple_of((q ^ k) * width, width), width)
        two[:, cols] = piece[...]
    lanes = blocks.shape[2]
    for b in range(16):
        one[:, b * lanes : (b + 1) * lanes] = blocks[b]


def unsplit(q, blocks, pieces):
    rows, width = pieces[0].shape
    shape = jax.ShapeDtypeStruct((rows, 4 * width), pieces[0].dtype)
    return pl.pallas_call(
        unsplit_kernel,
        out_shape=[shape] * 2,
        in_specs=[spec(SMEM)] + [spec()] * 5,
        out_specs=[spec()] * 2,
        compiler_params=pltpu.CompilerParams(vmem_limit_bytes=SMALL),
        name="unsplit",
    )(q, blocks, *pieces)


def line(col):
    return jnp.broadcast_to(col, (col.shape[0], 128)).T[0:1, :]


def chunk(buffer, *at):
    blocks = [buffer[(h,) + at] for h in range(4)]
    return jnp.concatenate([block.reshape(-1, block.shape[-1]) for block in blocks], 1)


def back(own, other, weight, own_at, other_at, vec):
    mean_own, inv_own, proj_own = (vec[own_at + i : own_at + i + 1, :] for i in range(3))
    mean_other, inv_other = (vec[other_at + i : other_at + i + 1, :] for i in range(2))
    rounded = ((other.astype(jnp.float32) - mean_other) * inv_other).astype(jnp.bfloat16)
    product = jnp.dot(rounded, weight, preferred_element_type=jnp.float32)
    slant = inv_own * inv_own * proj_own
    return (inv_own * product - (own.astype(jnp.float32) - mean_own) * slant).astype(jnp.bfloat16)


def moments(total, square, count):
    mean = jnp.sum(total, 0, keepdims=True) / count
    inverse = lax.rsqrt(jnp.sum(square, 0, keepdims=True) / count - mean * mean + EPSILON)
    return mean, inverse


def finish(count, pos, acc, sums, lanes, cols, slope_out, turned, vec_out):
    for at in range(2):
        mean, inverse = moments(sums[2 * at], sums[2 * at + 1], count)
        vec_out[3 * at : 3 * at + 1, :] = mean
        vec_out[3 * at + 1 : 3 * at + 2, :] = inverse
    vec_out[5:8, :] = jnp.zeros((3, acc.shape[1]), jnp.float32)
    cols[...] = vec_out[...].T

    @pl.loop(0, 4)
    def _(r):
        rows = pl.ds(pl.multiple_of(r * lanes, lanes), lanes)
        mean_one, inv_one = cols[rows, 0:1], cols[rows, 1:2]
        mean_two, inv_two = vec_out[3:4, :], vec_out[4:5, :]
        corr = (acc[rows, :] / count - mean_one * mean_two) * (inv_one * inv_two)
        row = lax.broadcasted_iota(jnp.int32, corr.shape, 0)
        row += r * (16 * lanes) + (pos[0] * 4 + pos[1]) * lanes
        col = lax.broadcasted_iota(jnp.int32, corr.shape, 1) + pos[2] * corr.shape[1]
        slope = jnp.where(row == col, -2.0 * (1.0 - corr), 2.0 * OFF_WEIGHT * corr)
        weight = slope * corr
        vec_out[2:3, rows] = line(jnp.sum(weight, 1, keepdims=True))
        vec_out[5:6, :] += jnp.sum(weight, 0, keepdims=True)
        slope_out[rows, :] = slope.astype(jnp.bfloat16)
        turned[:, rows] = slope.T.astype(jnp.bfloat16)


def tile_kernel(count, places, pos, one, *refs):
    arrays, refs = refs[: len(places)], refs[len(places) :]
    part_out, slope_out, vec_out, buf_one, buf_two, acc, sums = refs[:7]
    cols, turned, parts, in_sem, out_sem = refs[7:]
    lanes = one.shape[-1]
    loads = [[], [], [], []]
    for q in range(4):
        for h in range(4):
            loads[q].append((one.at[h, q], buf_one.at[h, q]))
    for ref, place in zip(arrays, places):
        q, k, index = place
        if q < 2:
            target = buf_two.at[q, :, (pos[1] - k) % 4]
        else:
            target = buf_two.at[q, (pos[0] - k) % 4]
        loads[q].append((ref.at[index], target))
    loads = [
        [pltpu.make_async_copy(src, dst, in_sem.at[q, i]) for i, (src, dst) in enumerate(row)]
        for q, row in enumerate(loads)
    ]
    for row in loads:
        for copy in row:
            copy.start()
    acc[...] = jnp.zeros_like(acc)
    sums[...] = jnp.zeros_like(sums)

    @pl.loop(0, 4)
    def _(q):
        for h in range(4):
            pltpu.make_async_copy(buf_one.at[h, q], buf_one.at[h, q], in_sem.at[q, h]).wait()
            pltpu.make_async_copy(buf_two.at[q, h], buf_two.at[q, h], in_sem.at[q, 4 + h]).wait()

        @pl.loop(0, 4, unroll=4)
        def _(y):
            left = chunk(buf_one, q, slice(None), y)
            right = buf_two[q, :, y].reshape(left.shape)
            acc[...] += lax.dot_general(
                left, right, (((0,), (0,)), ((), ())), preferred_element_type=jnp.float32
            )
            for at, block in ((0, left), (2, right)):
                value = block.astype(jnp.float32).reshape(block.shape[0] // 8, 8, block.shape[1])
                sums[at] += jnp.sum(value, 0)
                sums[at + 1] += jnp.sum(value * value, 0)

    finish(count, pos, acc, sums, lanes, cols, slope_out, turned, vec_out)

    def write(step, h):
        rows = part_out.at[h, step // 4, :, step % 4]
        return pltpu.make_async_copy(parts.at[step % 4, h], rows, out_sem.at[step % 4, h])

    @pl.loop(0, 16)
    def _(step):
        @pl.when(step >= 4)
        def _():
            for h in range(4):
                write(step - 4, h).wait()

        q, y = step // 4, step % 4
        own = chunk(buf_one, q, slice(None), y)
        other = buf_two[q, :, y].reshape(own.shape)
        part = back(own, other, turned[...], 0, 3, vec_out)
        for h in range(4):
            block = part[:, h * lanes : (h + 1) * lanes]
            parts[step % 4, h] = block.reshape(parts.shape[2:])
            write(step, h).start()

    for step in range(12, 16):
        for h in range(4):
            write(step, h).wait()


def tile_work(pos, one, pieces):
    rows, lanes = one.shape[4:]
    width = 4 * lanes
    count = 64 * rows
    arrays, places = [], []
    for at in range(8):
        for part in range(2):
            array, index = pieces[at][part]
            arrays.append(array)
            places.append((2 * (at // 4) + part, at % 4, index))
    anywhere = pl.BlockSpec(memory_space=pl.ANY)
    return pl.pallas_call(
        functools.partial(tile_kernel, count, places),
        in_specs=[spec(SMEM)] + [anywhere] * 17,
        out_specs=[anywhere, spec(), spec()],
        out_shape=[
            jax.ShapeDtypeStruct(one.shape, jnp.bfloat16),
            jax.ShapeDtypeStruct((width, width), jnp.bfloat16),
            jax.ShapeDtypeStruct((8, width), jnp.float32),
        ],
        scratch_shapes=[
            VMEM((4, 4, 4, 4, rows, lanes), jnp.bfloat16),
            VMEM((4, 4, 4, rows, width), jnp.bfloat16),
            VMEM((width, width), jnp.float32),
            VMEM((4, 8, width), jnp.float32),
            VMEM((width, 8), jnp.float32),
            VMEM((width, width), jnp.bfloat16),
            VMEM((4, 4, 4, rows, lanes), jnp.bfloat16),
            pltpu.SemaphoreType.DMA((4, 8)),
            pltpu.SemaphoreType.DMA((4, 4)),
        ],
        cost_estimate=pl.CostEstimate(
            flops=4 * count * width * width, bytes_accessed=6 * count * width, transcendentals=0
        ),
        compiler_params=pltpu.CompilerParams(vmem_limit_bytes=LIMIT),
        name="tile",
    )(pos, one, *arrays)


def back_two_kernel(items, indices, pos, one, *refs):
    count = len(items)
    arrays, (weight, vec), refs = refs[:count], refs[count : count + 2], refs[count + 2 :]
    extras, outs, scratch = refs[: -count - 6], refs[-count - 6 : -6], refs[-6:]
    buf_one, buf_two, buf_extra, parts, in_sem, out_sem = scratch
    loads = []
    for i, (half, part, k) in enumerate(items):
        q = 2 * half + part
        row = []
        for h in range(4):
            if half == 0:
                rows = one.at[h, q, :, (pos[1] + k) % 4]
            else:
                rows = one.at[h, q, (pos[0] + k) % 4]
            row.append((rows, buf_one.at[h, i]))
        row.append((arrays[i].at[indices[i]], buf_two.at[i]))
        if extras:
            row.append((extras[i].at[0], buf_extra.at[i]))
        loads.append(
            [pltpu.make_async_copy(src, dst, in_sem.at[i, j]) for j, (src, dst) in enumerate(row)]
        )
    for row in loads:
        for copy in row:
            copy.start()

    @pl.loop(0, count)
    def _(i):
        for h in range(4):
            pltpu.make_async_copy(buf_one.at[h, i], buf_one.at[h, i], in_sem.at[i, h]).wait()
        pltpu.make_async_copy(buf_two.at[i], buf_two.at[i], in_sem.at[i, 4]).wait()
        if extras:
            pltpu.make_async_copy(buf_extra.at[i], buf_extra.at[i], in_sem.at[i, 5]).wait()
        other = chunk(buf_one, i)
        own = buf_two[i].reshape(other.shape)
        value = back(own, other, weight[...], 3, 0, vec)
        if extras:
            value = total(value, buf_extra[i].reshape(other.shape))
        parts[i] = value.reshape(parts.shape[1:])
        for n in range(count):

            @pl.when(i == n)
            def _():
                pltpu.make_async_copy(parts.at[n], outs[n].at[0], out_sem.at[n]).start()

    for n in range(count):
        pltpu.make_async_copy(parts.at[n], outs[n].at[0], out_sem.at[n]).wait()


def back_two(pos, one, pieces, weight, vec, items, extras=()):
    rows, lanes = one.shape[4:]
    width = 4 * lanes
    count = len(items)
    mine = [pieces[4 * half + -k % 4][part] for half, part, k in items]
    anywhere = pl.BlockSpec(memory_space=pl.ANY)
    return pl.pallas_call(
        functools.partial(back_two_kernel, items, [piece[1] for piece in mine]),
        in_specs=[spec(SMEM)] + [anywhere] * (1 + count) + [spec()] * 2 + [anywhere] * len(extras),
        out_specs=[anywhere] * count,
        out_shape=[jax.ShapeDtypeStruct((1, 4, rows, width), jnp.bfloat16)] * count,
        scratch_shapes=[
            VMEM((4, count, 4, rows, lanes), jnp.bfloat16),
            VMEM((count, 4, rows, width), jnp.bfloat16),
            VMEM((count, 4, rows, width), jnp.bfloat16),
            VMEM((count, 4, rows, width), jnp.bfloat16),
            pltpu.SemaphoreType.DMA((count, 6)),
            pltpu.SemaphoreType.DMA((count,)),
        ],
        cost_estimate=pl.CostEstimate(
            flops=8 * count * rows * width * width,
            bytes_accessed=24 * count * rows * width,
            transcendentals=0,
        ),
        compiler_params=pltpu.CompilerParams(vmem_limit_bytes=LIMIT),
        name="back_two",
    )(pos, one, *[piece[0] for piece in mine], weight, vec, *extras)


def gather_ring(value, axis):
    behind = lax.ppermute(value, axis, shift(1))
    ahead = lax.ppermute(value, axis, shift(3))
    far = [
        lax.ppermute(behind[0:1], axis, shift(1)),
        lax.ppermute(ahead[1:2], axis, shift(3)),
    ]
    return [[(value, 0), (value, 1)], [(behind, 0), (behind, 1)], [(far[0], 0), (far[1], 0)]] + [
        [(ahead, 0), (ahead, 1)]
    ]


def put(buffer, piece, index):
    return lax.dynamic_update_index_in_dim(buffer, piece, index, 1)


def local(view_one, view_two):
    x, y = lax.axis_index("x"), lax.axis_index("y")
    zl, c, zh = lax.axis_index("zl"), lax.axis_index("c"), lax.axis_index("zh")
    slot = zl * 2 + c
    q = slot.astype(jnp.int32).reshape(1)
    pos = jnp.stack([x, y, zh * 4 + slot]).astype(jnp.int32)
    rows = view_one.shape[0]
    width = view_one.shape[1] // 4
    lanes = width // 4
    with jax.named_scope("relayout"):
        blocks, *pieces = split(q, view_one, view_two)
        for k in (1, 2, 3):
            pieces[k] = lax.ppermute(pieces[k], AXES, near(k))
        own_one = lax.all_to_all(blocks, ("x", "y"), 0, 0, tiled=True)
        a, b = join(q, pieces)
        own_one, a, b = lax.optimization_barrier((own_one, a, b))
    with jax.named_scope("gather_one"):
        first = lax.all_gather(own_one.reshape(16 * rows, lanes), COLS, tiled=True)
    with jax.named_scope("gather_two"):
        low = jnp.zeros((2, 4, rows, width), view_two.dtype)
        high = jnp.zeros((2, 4, rows, width), view_two.dtype)
        for k in (0, 1, 3, 2):
            low = put(low, lax.ppermute(a, "x", shift(k)) if k else a, (x - k) % 4)
            high = put(high, lax.ppermute(b, "y", shift(k)) if k else b, (y - k) % 4)
        low, high = lax.optimization_barrier((low, high))
        gathered = gather_ring(low, "y") + gather_ring(high, "x")
    first = first.reshape(4, 4, 4, 4, rows, lanes)
    part_one, slope, vec = tile_work(pos, first, gathered)
    with jax.named_scope("scatter_one"):
        grad_one = lax.psum_scatter(part_one.reshape(256 * rows, lanes), COLS, tiled=True)
    with jax.named_scope("scatter_two"):
        axes = ("y", "x")
        work = functools.partial(back_two, pos, first, gathered, slope, vec)

        def send(values, items):
            return [
                lax.ppermute(value, axes[half], shift(k))
                for value, (half, _, k) in zip(values, items)
            ]

        far = work([(0, 0, 2), (0, 1, 2), (1, 0, 2), (1, 1, 2)])
        plain_items = [(0, 0, 3), (0, 1, 1), (1, 0, 3), (1, 1, 1)]
        added_items = [(0, 0, 1), (0, 1, 3), (1, 0, 1), (1, 1, 3)]
        far = send(far, added_items)
        plain = send(work(plain_items), plain_items)
        added = send(work(added_items, far), added_items)
        own = work([(0, 0, 0), (0, 1, 0), (1, 0, 0), (1, 1, 0)])
        low = list(sum_pick(pos[0:1], [own[0], plain[0], added[0], own[1], plain[1], added[1]]))
        high = list(sum_pick(pos[1:2], [own[2], plain[2], added[2], own[3], plain[3], added[3]]))
        for k in (1, 3, 2):
            low[k] = lax.ppermute(low[k], "x", shift(k))
            high[k] = lax.ppermute(high[k], "y", shift(k))
    with jax.named_scope("relayout_back"):
        pieces = list(unjoin(q, low, high))
        for k in (1, 2, 3):
            pieces[k] = lax.ppermute(pieces[k], AXES, near(k))
        grad_one, *pieces = lax.optimization_barrier((grad_one, *pieces))
        grad_one = lax.all_to_all(grad_one.reshape(16, rows, lanes), ("x", "y"), 0, 0, tiled=True)
        return tuple(unsplit(q, grad_one, pieces))


def solution(mesh):
    grid = Mesh(mesh.devices.reshape(SIZES), AXES)
    spread = P(("x", "zl", "y", "c"), "zh")
    return jax.shard_map(
        local, mesh=grid, in_specs=(spread, spread), out_specs=(spread, spread), check_vma=False
    )
```

```python
import functools
import itertools

import jax
import jax.numpy as jnp
from jax import lax
from jax.experimental import pallas as pl
from jax.experimental.pallas import tpu as pltpu
from jax.sharding import Mesh
from jax.sharding import PartitionSpec as P

EPSILON = 1e-05
OFF_WEIGHT = 0.0051
SIZES = (4, 2, 4, 2, 4)
AXES = ("x", "zl", "y", "c", "zh")
COLS = ("zh", "zl", "c")
VMEM = pltpu.VMEM
LIMIT = 58 * 2**20
SMALL = 12 * 2**20
SMEM = pltpu.SMEM


def device(x, zl, y, c, zh):
    return (((x * 2 + zl) * 4 + y) * 2 + c) * 4 + zh


def near(k):
    out = []
    for x, zl, y, c, zh in itertools.product(*map(range, SIZES)):
        q = (zl * 2 + c) ^ k
        out.append((device(x, zl, y, c, zh), device(x, q // 2, y, q % 2, zh)))
    return out


def shift(k):
    return [(i, (i + k) % 4) for i in range(4)]


def spec(space=VMEM):
    return pl.BlockSpec(memory_space=space)


def split_kernel(q_ref, one, two, blocks, *outs):
    q = q_ref[0]
    width = two.shape[1] // 4
    for k, out in enumerate(outs):
        cols = pl.ds(pl.multiple_of((q ^ k) * width, width), width)
        out[...] = two[:, cols]
    lanes = blocks.shape[2]
    for b in range(16):
        blocks[b] = one[:, b * lanes : (b + 1) * lanes]


def split(q, one, two):
    rows, width = one.shape
    shape = jax.ShapeDtypeStruct((rows, width // 4), one.dtype)
    return pl.pallas_call(
        split_kernel,
        out_shape=[jax.ShapeDtypeStruct((16, rows, width // 16), one.dtype)] + [shape] * 4,
        in_specs=[spec(SMEM), spec(), spec()],
        out_specs=[spec()] * 5,
        compiler_params=pltpu.CompilerParams(vmem_limit_bytes=SMALL),
        name="split",
    )(q, one, two)


def join_kernel(q_ref, p0, p1, p2, p3, low, high):
    q = q_ref[0]
    for k, piece in enumerate((p0, p1, p2, p3)):
        at = q ^ k

        @pl.when(at < 2)
        def _():
            low[at & 1] = piece[...]

        @pl.when(at >= 2)
        def _():
            high[at & 1] = piece[...]


def join(q, pieces):
    shape = jax.ShapeDtypeStruct((2,) + pieces[0].shape, pieces[0].dtype)
    return pl.pallas_call(
        join_kernel,
        out_shape=[shape] * 2,
        in_specs=[spec(SMEM)] + [spec()] * 4,
        out_specs=[spec()] * 2,
        compiler_params=pltpu.CompilerParams(vmem_limit_bytes=SMALL),
        name="join",
    )(q, *pieces)


def total(*refs):
    return functools.reduce(jnp.add, [ref.astype(jnp.float32) for ref in refs]).astype(jnp.bfloat16)


def sum_pick_kernel(me, *refs):
    for k, out in enumerate(refs[6:]):
        at = (me[0] + k) % 4
        out[0] = total(*[ref[0, at] for ref in refs[:3]])
        out[1] = total(*[ref[0, at] for ref in refs[3:6]])


def sum_pick(me, terms):
    _, _, rows, width = terms[0].shape
    return pl.pallas_call(
        sum_pick_kernel,
        out_shape=[jax.ShapeDtypeStruct((2, rows, width), jnp.bfloat16)] * 4,
        in_specs=[spec(SMEM)] + [spec()] * 6,
        out_specs=[spec()] * 4,
        compiler_params=pltpu.CompilerParams(vmem_limit_bytes=SMALL),
        name="sum_pick",
    )(me, *terms)


def unjoin_kernel(q_ref, *refs):
    q = q_ref[0]
    low, high, outs = refs[:4], refs[4:8], refs[8:]
    for k, out in enumerate(outs):
        at = q ^ k

        @pl.when(at < 2)
        def _():
            out[...] = total(*[ref[at & 1] for ref in low])

        @pl.when(at >= 2)
        def _():
            out[...] = total(*[ref[at & 1] for ref in high])


def unjoin(q, low, high):
    return pl.pallas_call(
        unjoin_kernel,
        out_shape=[jax.ShapeDtypeStruct(low[0].shape[1:], jnp.bfloat16)] * 4,
        in_specs=[spec(SMEM)] + [spec()] * 8,
        out_specs=[spec()] * 4,
        compiler_params=pltpu.CompilerParams(vmem_limit_bytes=SMALL),
        name="unjoin",
    )(q, *low, *high)


def unsplit_kernel(q_ref, blocks, p0, p1, p2, p3, one, two):
    q = q_ref[0]
    width = p0.shape[1]
    for k, piece in enumerate((p0, p1, p2, p3)):
        cols = pl.ds(pl.multiple_of((q ^ k) * width, width), width)
        two[:, cols] = piece[...]
    lanes = blocks.shape[2]
    for b in range(16):
        one[:, b * lanes : (b + 1) * lanes] = blocks[b]


def unsplit(q, blocks, pieces):
    rows, width = pieces[0].shape
    shape = jax.ShapeDtypeStruct((rows, 4 * width), pieces[0].dtype)
    return pl.pallas_call(
        unsplit_kernel,
        out_shape=[shape] * 2,
        in_specs=[spec(SMEM)] + [spec()] * 5,
        out_specs=[spec()] * 2,
        compiler_params=pltpu.CompilerParams(vmem_limit_bytes=SMALL),
        name="unsplit",
    )(q, blocks, *pieces)


def line(col):
    return jnp.broadcast_to(col, (col.shape[0], 128)).T[0:1, :]


def chunk(buffer, *at):
    blocks = [buffer[(h,) + at] for h in range(4)]
    return jnp.concatenate([block.reshape(-1, block.shape[-1]) for block in blocks], 1)


def back(own, other, weight, own_at, other_at, vec):
    mean_own, inv_own, proj_own = (vec[own_at + i : own_at + i + 1, :] for i in range(3))
    mean_other, inv_other = (vec[other_at + i : other_at + i + 1, :] for i in range(2))
    rounded = ((other.astype(jnp.float32) - mean_other) * inv_other).astype(jnp.bfloat16)
    product = jnp.dot(rounded, weight, preferred_element_type=jnp.float32)
    slant = inv_own * inv_own * proj_own
    return (inv_own * product - (own.astype(jnp.float32) - mean_own) * slant).astype(jnp.bfloat16)


def moments(total, square, count):
    mean = jnp.sum(total, 0, keepdims=True) / count
    inverse = lax.rsqrt(jnp.sum(square, 0, keepdims=True) / count - mean * mean + EPSILON)
    return mean, inverse


def finish(count, pos, acc, sums, lanes, cols, slope_out, turned, vec_out):
    for at in range(2):
        mean, inverse = moments(sums[2 * at], sums[2 * at + 1], count)
        vec_out[3 * at : 3 * at + 1, :] = mean
        vec_out[3 * at + 1 : 3 * at + 2, :] = inverse
    vec_out[5:8, :] = jnp.zeros((3, acc.shape[1]), jnp.float32)
    cols[...] = vec_out[...].T

    @pl.loop(0, 4)
    def _(r):
        rows = pl.ds(pl.multiple_of(r * lanes, lanes), lanes)
        mean_one, inv_one = cols[rows, 0:1], cols[rows, 1:2]
        mean_two, inv_two = vec_out[3:4, :], vec_out[4:5, :]
        corr = (acc[rows, :] / count - mean_one * mean_two) * (inv_one * inv_two)
        row = lax.broadcasted_iota(jnp.int32, corr.shape, 0)
        row += r * (16 * lanes) + (pos[0] * 4 + pos[1]) * lanes
        col = lax.broadcasted_iota(jnp.int32, corr.shape, 1) + pos[2] * corr.shape[1]
        slope = jnp.where(row == col, -2.0 * (1.0 - corr), 2.0 * OFF_WEIGHT * corr)
        weight = slope * corr
        vec_out[2:3, rows] = line(jnp.sum(weight, 1, keepdims=True))
        vec_out[5:6, :] += jnp.sum(weight, 0, keepdims=True)
        slope_out[rows, :] = slope.astype(jnp.bfloat16)
        turned[:, rows] = slope.T.astype(jnp.bfloat16)


def tile_kernel(count, places, pos, one, *refs):
    arrays, refs = refs[: len(places)], refs[len(places) :]
    part_out, slope_out, vec_out, buf_one, buf_two, acc, sums = refs[:7]
    cols, turned, parts, in_sem, out_sem = refs[7:]
    lanes = one.shape[-1]
    loads = [[], [], [], []]
    for q in range(4):
        for h in range(4):
            loads[q].append((one.at[h, q], buf_one.at[h, q]))
    for ref, place in zip(arrays, places):
        q, k, index = place
        if q < 2:
            target = buf_two.at[q, :, (pos[1] - k) % 4]
        else:
            target = buf_two.at[q, (pos[0] - k) % 4]
        loads[q].append((ref.at[index], target))
    loads = [
        [pltpu.make_async_copy(src, dst, in_sem.at[q, i]) for i, (src, dst) in enumerate(row)]
        for q, row in enumerate(loads)
    ]
    for row in loads:
        for copy in row:
            copy.start()
    acc[...] = jnp.zeros_like(acc)
    sums[...] = jnp.zeros_like(sums)

    @pl.loop(0, 4)
    def _(q):
        for h in range(4):
            pltpu.make_async_copy(buf_one.at[h, q], buf_one.at[h, q], in_sem.at[q, h]).wait()
            pltpu.make_async_copy(buf_two.at[q, h], buf_two.at[q, h], in_sem.at[q, 4 + h]).wait()

        @pl.loop(0, 4, unroll=4)
        def _(y):
            left = chunk(buf_one, q, slice(None), y)
            right = buf_two[q, :, y].reshape(left.shape)
            acc[...] += lax.dot_general(
                left, right, (((0,), (0,)), ((), ())), preferred_element_type=jnp.float32
            )
            for at, block in ((0, left), (2, right)):
                value = block.astype(jnp.float32).reshape(block.shape[0] // 8, 8, block.shape[1])
                sums[at] += jnp.sum(value, 0)
                sums[at + 1] += jnp.sum(value * value, 0)

    finish(count, pos, acc, sums, lanes, cols, slope_out, turned, vec_out)

    def write(step, h):
        rows = part_out.at[h, step // 4, :, step % 4]
        return pltpu.make_async_copy(parts.at[step % 4, h], rows, out_sem.at[step % 4, h])

    @pl.loop(0, 16)
    def _(step):
        @pl.when(step >= 4)
        def _():
            for h in range(4):
                write(step - 4, h).wait()

        q, y = step // 4, step % 4
        own = chunk(buf_one, q, slice(None), y)
        other = buf_two[q, :, y].reshape(own.shape)
        part = back(own, other, turned[...], 0, 3, vec_out)
        for h in range(4):
            block = part[:, h * lanes : (h + 1) * lanes]
            parts[step % 4, h] = block.reshape(parts.shape[2:])
            write(step, h).start()

    for step in range(12, 16):
        for h in range(4):
            write(step, h).wait()


def tile_work(pos, one, pieces):
    rows, lanes = one.shape[4:]
    width = 4 * lanes
    count = 64 * rows
    arrays, places = [], []
    for at in range(8):
        for part in range(2):
            array, index = pieces[at][part]
            arrays.append(array)
            places.append((2 * (at // 4) + part, at % 4, index))
    anywhere = pl.BlockSpec(memory_space=pl.ANY)
    return pl.pallas_call(
        functools.partial(tile_kernel, count, places),
        in_specs=[spec(SMEM)] + [anywhere] * 17,
        out_specs=[anywhere, spec(), spec()],
        out_shape=[
            jax.ShapeDtypeStruct(one.shape, jnp.bfloat16),
            jax.ShapeDtypeStruct((width, width), jnp.bfloat16),
            jax.ShapeDtypeStruct((8, width), jnp.float32),
        ],
        scratch_shapes=[
            VMEM((4, 4, 4, 4, rows, lanes), jnp.bfloat16),
            VMEM((4, 4, 4, rows, width), jnp.bfloat16),
            VMEM((width, width), jnp.float32),
            VMEM((4, 8, width), jnp.float32),
            VMEM((width, 8), jnp.float32),
            VMEM((width, width), jnp.bfloat16),
            VMEM((4, 4, 4, rows, lanes), jnp.bfloat16),
            pltpu.SemaphoreType.DMA((4, 8)),
            pltpu.SemaphoreType.DMA((4, 4)),
        ],
        cost_estimate=pl.CostEstimate(
            flops=4 * count * width * width, bytes_accessed=6 * count * width, transcendentals=0
        ),
        compiler_params=pltpu.CompilerParams(vmem_limit_bytes=LIMIT),
        name="tile",
    )(pos, one, *arrays)


def back_two_kernel(items, indices, pos, one, *refs):
    count = len(items)
    arrays, (weight, vec), refs = refs[:count], refs[count : count + 2], refs[count + 2 :]
    extras, outs, scratch = refs[: -count - 6], refs[-count - 6 : -6], refs[-6:]
    buf_one, buf_two, buf_extra, parts, in_sem, out_sem = scratch
    loads = []
    for i, (half, part, k) in enumerate(items):
        q = 2 * half + part
        row = []
        for h in range(4):
            if half == 0:
                rows = one.at[h, q, :, (pos[1] + k) % 4]
            else:
                rows = one.at[h, q, (pos[0] + k) % 4]
            row.append((rows, buf_one.at[h, i]))
        row.append((arrays[i].at[indices[i]], buf_two.at[i]))
        if extras:
            row.append((extras[i].at[0], buf_extra.at[i]))
        loads.append(
            [pltpu.make_async_copy(src, dst, in_sem.at[i, j]) for j, (src, dst) in enumerate(row)]
        )
    for row in loads:
        for copy in row:
            copy.start()

    @pl.loop(0, count)
    def _(i):
        for h in range(4):
            pltpu.make_async_copy(buf_one.at[h, i], buf_one.at[h, i], in_sem.at[i, h]).wait()
        pltpu.make_async_copy(buf_two.at[i], buf_two.at[i], in_sem.at[i, 4]).wait()
        if extras:
            pltpu.make_async_copy(buf_extra.at[i], buf_extra.at[i], in_sem.at[i, 5]).wait()
        other = chunk(buf_one, i)
        own = buf_two[i].reshape(other.shape)
        value = back(own, other, weight[...], 3, 0, vec)
        if extras:
            value = total(value, buf_extra[i].reshape(other.shape))
        parts[i] = value.reshape(parts.shape[1:])
        for n in range(count):

            @pl.when(i == n)
            def _():
                pltpu.make_async_copy(parts.at[n], outs[n].at[0], out_sem.at[n]).start()

    for n in range(count):
        pltpu.make_async_copy(parts.at[n], outs[n].at[0], out_sem.at[n]).wait()


def back_two(pos, one, pieces, weight, vec, items, extras=()):
    rows, lanes = one.shape[4:]
    width = 4 * lanes
    count = len(items)
    mine = [pieces[4 * half + -k % 4][part] for half, part, k in items]
    anywhere = pl.BlockSpec(memory_space=pl.ANY)
    return pl.pallas_call(
        functools.partial(back_two_kernel, items, [piece[1] for piece in mine]),
        in_specs=[spec(SMEM)] + [anywhere] * (1 + count) + [spec()] * 2 + [anywhere] * len(extras),
        out_specs=[anywhere] * count,
        out_shape=[jax.ShapeDtypeStruct((1, 4, rows, width), jnp.bfloat16)] * count,
        scratch_shapes=[
            VMEM((4, count, 4, rows, lanes), jnp.bfloat16),
            VMEM((count, 4, rows, width), jnp.bfloat16),
            VMEM((count, 4, rows, width), jnp.bfloat16),
            VMEM((count, 4, rows, width), jnp.bfloat16),
            pltpu.SemaphoreType.DMA((count, 6)),
            pltpu.SemaphoreType.DMA((count,)),
        ],
        cost_estimate=pl.CostEstimate(
            flops=8 * count * rows * width * width,
            bytes_accessed=24 * count * rows * width,
            transcendentals=0,
        ),
        compiler_params=pltpu.CompilerParams(vmem_limit_bytes=LIMIT),
        name="back_two",
    )(pos, one, *[piece[0] for piece in mine], weight, vec, *extras)


def gather_ring(value, axis):
    behind = lax.ppermute(value, axis, shift(1))
    ahead = lax.ppermute(value, axis, shift(3))
    far = [
        lax.ppermute(behind[0:1], axis, shift(1)),
        lax.ppermute(ahead[1:2], axis, shift(3)),
    ]
    return [[(value, 0), (value, 1)], [(behind, 0), (behind, 1)], [(far[0], 0), (far[1], 0)]] + [
        [(ahead, 0), (ahead, 1)]
    ]


def put(buffer, piece, index):
    return lax.dynamic_update_index_in_dim(buffer, piece, index, 1)


def local(view_one, view_two):
    x, y = lax.axis_index("x"), lax.axis_index("y")
    zl, c, zh = lax.axis_index("zl"), lax.axis_index("c"), lax.axis_index("zh")
    slot = zl * 2 + c
    q = slot.astype(jnp.int32).reshape(1)
    pos = jnp.stack([x, y, zh * 4 + slot]).astype(jnp.int32)
    rows = view_one.shape[0]
    width = view_one.shape[1] // 4
    lanes = width // 4
    with jax.named_scope("relayout"):
        blocks, *pieces = split(q, view_one, view_two)
        for k in (1, 2, 3):
            pieces[k] = lax.ppermute(pieces[k], AXES, near(k))
        own_one = lax.all_to_all(blocks, ("x", "y"), 0, 0, tiled=True)
        a, b = join(q, pieces)
        own_one, a, b = lax.optimization_barrier((own_one, a, b))
    with jax.named_scope("gather_one"):
        first = lax.all_gather(own_one.reshape(16 * rows, lanes), COLS, tiled=True)
    with jax.named_scope("gather_two"):
        low = jnp.zeros((2, 4, rows, width), view_two.dtype)
        high = jnp.zeros((2, 4, rows, width), view_two.dtype)
        for k in (0, 1, 3, 2):
            low = put(low, lax.ppermute(a, "x", shift(k)) if k else a, (x - k) % 4)
            high = put(high, lax.ppermute(b, "y", shift(k)) if k else b, (y - k) % 4)
        low, high = lax.optimization_barrier((low, high))
        gathered = gather_ring(low, "y") + gather_ring(high, "x")
    first = first.reshape(4, 4, 4, 4, rows, lanes)
    part_one, slope, vec = tile_work(pos, first, gathered)
    with jax.named_scope("scatter_one"):
        grad_one = lax.psum_scatter(part_one.reshape(256 * rows, lanes), COLS, tiled=True)
    with jax.named_scope("scatter_two"):
        axes = ("y", "x")
        work = functools.partial(back_two, pos, first, gathered, slope, vec)

        def send(values, items):
            return [
                lax.ppermute(value, axes[half], shift(k))
                for value, (half, _, k) in zip(values, items)
            ]

        far = work([(0, 0, 2), (0, 1, 2), (1, 0, 2), (1, 1, 2)])
        plain_items = [(0, 0, 3), (0, 1, 1), (1, 0, 3), (1, 1, 1)]
        added_items = [(0, 0, 1), (0, 1, 3), (1, 0, 1), (1, 1, 3)]
        far = send(far, added_items)
        plain = send(work(plain_items), plain_items)
        own = work([(0, 0, 0), (0, 1, 0), (1, 0, 0), (1, 1, 0)])
        own, far = lax.optimization_barrier((list(own), far))
        added = send(work(added_items, far), added_items)
        low = list(sum_pick(pos[0:1], [own[0], plain[0], added[0], own[1], plain[1], added[1]]))
        high = list(sum_pick(pos[1:2], [own[2], plain[2], added[2], own[3], plain[3], added[3]]))
        for k in (1, 3, 2):
            low[k] = lax.ppermute(low[k], "x", shift(k))
            high[k] = lax.ppermute(high[k], "y", shift(k))
    with jax.named_scope("relayout_back"):
        pieces = list(unjoin(q, low, high))
        for k in (1, 2, 3):
            pieces[k] = lax.ppermute(pieces[k], AXES, near(k))
        grad_one, pieces[1] = lax.optimization_barrier((grad_one, pieces[1]))
        grad_one = lax.all_to_all(grad_one.reshape(16, rows, lanes), ("x", "y"), 0, 0, tiled=True)
        return tuple(unsplit(q, grad_one, pieces))


def solution(mesh):
    grid = Mesh(mesh.devices.reshape(SIZES), AXES)
    spread = P(("x", "zl", "y", "c"), "zh")
    return jax.shard_map(
        local, mesh=grid, in_specs=(spread, spread), out_specs=(spread, spread), check_vma=False
    )
```
